32 devices in a mesh: seq: 8 (over z, x), tp: 4 (over y, core).
Axes of the slice: x: 2, y: 2, z: 4, core: 2. Of those that a mesh axis runs over, the one named last changes fastest.
Arguments:
- resp_rows: bfloat16 [128, 16, 5120], P('seq', None, 'tp'), may hold values from -6 to 6
- resp_len: int32 [128], replicated, may hold values from 1 to 16, as said below
- resp_shard: int32 [128, 1], replicated, may hold values from 0 to 7; in each aligned block of 16 rows (0 to 15, 16 to 31, ...) at most 2 rows name the same one
- group_prompt: int32 [8], replicated, may hold values from 0 to 7, each once
- prompt_kv: bfloat16 [2, 8, 256, 1024], P(None, 'seq', None, 'tp'), may hold values from -72 to 72
- w_query: bfloat16 [5120, 3072], P(None, 'tp'), may hold values from -0.078125 to 0.078125
- w_keyval: bfloat16 [2, 5120, 1024], P(None, None, 'tp'), may hold values from -0.078125 to 0.078125
- w_out: bfloat16 [3072, 5120], P('tp'), may hold values from -0.109375 to 0.109375
Outputs:
- attended: bfloat16 [128, 16, 5120], P('seq', None, 'tp')
The draws below stay inside these ranges and needn't reach their ends.
Inputs may be any that keep to these rules, and one draw needn't show every extreme that they name: `resp_shard`: in the rows of one device (one group) no learner appears more than 2 times, a bound that some block reaches. `group_prompt`: each prompt is answered by exactly one group. `resp_len`: some response has the full 16 tokens.
All inputs are finite; a program needn't handle non-finite values.
Results may differ from the reference program's by a relative error of at most 0.018.
Values may be sent and summed in bfloat16 or wider, within the bound.
A program may use at most 128 MiB of HBM per device.

```python
import math
import jax
import jax.numpy as jnp
import numpy as np
from jax import lax

D = 5120
HEADS = 24
KVH = 8
HD = 128
PL = 256
RMAX = 16
RESP_DEV = 16
CAP = 2
SLOTS = 16
PROMPTS = 8
RESPONSES = 128
N_SEQ = 8
N_TP = 4


def draw_resp_len(key, part):
    key = jax.random.fold_in(key, 7)
    first_key, second_key, third_key = jax.random.split(key, 3)
    first = jax.random.randint(first_key, (RESPONSES,), 1, RMAX + 1)
    second = jax.random.randint(second_key, (RESPONSES,), 1, RMAX + 1)
    lengths = (first * second + RMAX - 1) // RMAX
    spot = jax.random.randint(third_key, (), 0, RESPONSES)
    return jnp.where(jnp.arange(RESPONSES) == spot, RMAX, lengths).astype(jnp.int32)


def draw_prompt_kv(key, part):
    key = jax.random.fold_in(key, 11)
    base_key = jax.random.fold_in(key, 0)
    cache = jax.random.truncated_normal(base_key, -6.0, 6.0, (2, PROMPTS, PL, KVH * HD), jnp.float32)
    return cache.astype(jnp.bfloat16)


def block_scale(rng, dims, pieces, least, largest):
    def one(dim, shards_of):
        steps = jax.random.uniform(jax.random.fold_in(jax.random.fold_in(rng, 6), dim), (shards_of,), jnp.float32, least / len(pieces), largest / len(pieces))
        return jnp.repeat(jnp.exp(steps), dims[dim] // shards_of).reshape((-1,) + (1,) * (len(dims) - dim - 1))

    loudness = one(*pieces[0])
    for cut in pieces[1:]:
        loudness = loudness * one(*cut)
    return loudness


def deal_out(rng, own, number, rows, number_of, top, reach, slope):
    ranking = jax.random.permutation(rng, number_of)
    packed, usual = portions_of(number_of, rows * top, reach, slope, True), portions_of(number_of, rows * top, reach, slope, False)
    places = jnp.arange(number_of)

    def named(tallies, rotation):
        used = int((tallies > 0).sum())
        fixed = max(1, used // 4)
        shifted = fixed + (places - fixed + rotation * (used - fixed)) % max(1, number_of - fixed)
        return jnp.zeros((number_of,), jnp.int32).at[ranking[jnp.where(places < fixed, places, shifted)]].set(jnp.asarray(tallies, jnp.int32))

    tallies = jnp.where(number % 4 == 0, named(packed, number // 4), named(usual, number - number // 4 - 1))
    mixed = jax.random.permutation(jax.random.fold_in(own, 3), number_of)
    source_of, taker = mixed[0:number_of // 2 * 2:2], mixed[1:number_of // 2 * 2:2]
    room = jnp.minimum(tallies[source_of] - 1, reach - tallies[taker]) // 2
    room = jnp.where((source_of == ranking[0]) | (taker == ranking[0]) | (tallies[taker] == 0), 0, jnp.maximum(room, 0))
    shifted = jax.random.randint(jax.random.fold_in(own, 4), (number_of // 2,), 0, 1 << 20) % (room + 1)
    tallies = tallies.at[source_of].add(-shifted).at[taker].add(shifted)
    members = jnp.searchsorted(jnp.cumsum(tallies), jnp.arange(rows * top), side="right").astype(jnp.int32)
    listing = members.reshape(top, rows).T
    listing = listing[jax.random.permutation(jax.random.fold_in(own, 1), rows)]
    rotation = jax.random.randint(jax.random.fold_in(own, 2), (rows, 1), 0, top)
    return jnp.take_along_axis(listing, (jnp.arange(top)[None, :] + rotation) % top, axis=1)


def portions_of(count, total, most, lean, full):
    loads = [(1 << 20) // math.isqrt(standing ** lean) + 1 for standing in range(1, count + 1)]
    largest = most if full else min(most, max(-(-total // count), total * loads[0] // sum(loads)))
    least = 1 if total - largest >= count - 1 else 0
    holding, surplus = [largest] + [least] * (count - 1), total - largest - least * (count - 1)
    while surplus > 0:
        free = [i for i in range(1, count) if holding[i] < largest] or [i for i in range(1, count) if holding[i] < most]
        mass, remaining = sum([loads[i] for i in free]), surplus
        for i in free:
            more = min(most - holding[i], max(1, remaining * loads[i] // mass), surplus)
            holding[i] = holding[i] + more
            surplus = surplus - more
    return np.array(holding)


def gaussian(stream_key, shape, deviation, reach, shards=(), kind=jnp.bfloat16):
    level = block_scale(stream_key, shape, shards, -0.22, 0.18) if shards else 1.0
    result = jax.random.normal(stream_key, shape, jnp.float32) * deviation * level
    return jnp.minimum(jnp.maximum(result, -reach), reach).astype(kind)


def setup_inputs(seed: int = 0) -> dict:
    key_of = jax.random.split(jax.random.key(seed), 9)
    resp_rows = gaussian(key_of[0], (RESPONSES, RMAX, D), 1.0, 6.0, ((0, 8), (2, 4)))
    resp_len = draw_resp_len(jax.random.fold_in(key_of[8], 71), 0)
    resp_shard_keys = jax.random.split(jax.random.fold_in(key_of[2], 1), RESPONSES // RESP_DEV)
    resp_shard_turns = jax.random.permutation(jax.random.fold_in(key_of[2], 3), RESPONSES // RESP_DEV)
    resp_shard = jax.vmap(lambda own, number: deal_out(jax.random.fold_in(key_of[2], 2), own, number, RESP_DEV, N_SEQ, 1, CAP, 2))(resp_shard_keys, resp_shard_turns).reshape((RESPONSES, 1))
    group_prompt = jax.random.permutation(key_of[3], PROMPTS).astype(jnp.int32)
    prompt_kv = draw_prompt_kv(jax.random.fold_in(key_of[8], 71), 0)
    w_query = gaussian(key_of[5], (D, HEADS * HD), D ** -0.5, 0.078125, ((1, 4),))
    w_keyval = gaussian(key_of[6], (2, D, KVH * HD), D ** -0.5, 0.078125, ((2, 4),))
    w_out = gaussian(key_of[7], (HEADS * HD, D), (HEADS * HD) ** -0.5, 0.109375, ((0, 4),))
    return dict(resp_rows=resp_rows, resp_len=resp_len, resp_shard=resp_shard, group_prompt=group_prompt, prompt_kv=prompt_kv, w_query=w_query, w_keyval=w_keyval, w_out=w_out)


ROPE_BASE = 1000000.0

def rope_tables(count, width, offset):
    places = (offset + jnp.arange(count)).astype(jnp.float32)
    freqs = ROPE_BASE ** (-(jnp.arange(width // 2).astype(jnp.float32) * 2.0 / width))
    angles = places[:, None] * freqs[None, :]
    return (jnp.cos(angles), jnp.sin(angles))

def rotate(values, cosine, sine):
    half = values.shape[-1] // 2
    first = values[..., :half]
    second = values[..., half:]
    cosine = cosine[:, None, :]
    sine = sine[:, None, :]
    return jnp.concatenate([first * cosine - second * sine, second * cosine + first * sine], -1)

def attend(queries, own_keys, own_values, cached_keys, cached_values, lengths):
    scale = 1.0 / math.sqrt(queries.shape[-1])
    prior = jnp.einsum('stkrh,spkh->skrtp', queries.astype(jnp.float32), cached_keys.astype(jnp.float32)) * scale
    recent = jnp.einsum('stkrh,sukh->skrtu', queries.astype(jnp.float32), own_keys.astype(jnp.float32)) * scale
    places = jnp.arange(queries.shape[1])
    causal = places[:, None] >= places[None, :]
    recent = jnp.where(causal, recent, -1e+30)
    top = jnp.maximum(lax.optimization_barrier(jnp.max(prior, -1)), lax.optimization_barrier(jnp.max(recent, -1)))
    prior_exp = jnp.exp(prior - top[..., None])
    recent_exp = jnp.exp(recent - top[..., None])
    total = lax.optimization_barrier(jnp.sum(prior_exp, -1)) + lax.optimization_barrier(jnp.sum(recent_exp, -1))
    prior_w = (prior_exp / total[..., None]).astype(jnp.bfloat16)
    recent_w = (recent_exp / total[..., None]).astype(jnp.bfloat16)
    mixed = jnp.einsum('skrtp,spkh->stkrh', prior_w.astype(jnp.float32), cached_values.astype(jnp.float32))
    mixed = mixed + jnp.einsum('skrtu,sukh->stkrh', recent_w.astype(jnp.float32), own_values.astype(jnp.float32))
    valid = places[None, :] < lengths[:, None]
    mixed = jnp.where(valid[:, :, None, None, None], mixed, 0.0)
    return mixed.astype(jnp.bfloat16).reshape(queries.shape[0], queries.shape[1], -1)

def group_output(rows, cache, lengths, w_query, w_keyval, w_out):
    ratio = HEADS // KVH
    flat = rows.reshape(-1, D)
    cosine, sine = rope_tables(RMAX, HD, PL)
    queries = jnp.dot(flat, w_query, preferred_element_type=jnp.float32).reshape(RESP_DEV, RMAX, HEADS, HD)
    queries = rotate(queries, cosine, sine).astype(jnp.bfloat16).reshape(RESP_DEV, RMAX, KVH, ratio, HD)
    keys = jnp.dot(flat, w_keyval[0], preferred_element_type=jnp.float32).reshape(RESP_DEV, RMAX, KVH, HD)
    keys = rotate(keys, cosine, sine).astype(jnp.bfloat16)
    values = jnp.dot(flat, w_keyval[1], preferred_element_type=jnp.float32).astype(jnp.bfloat16).reshape(RESP_DEV, RMAX, KVH, HD)
    cached_keys = jnp.broadcast_to(cache[0].reshape(1, PL, KVH, HD), (RESP_DEV, PL, KVH, HD))
    cached_values = jnp.broadcast_to(cache[1].reshape(1, PL, KVH, HD), (RESP_DEV, PL, KVH, HD))
    attn = attend(queries, keys, values, cached_keys, cached_values, lengths).reshape(-1, HEADS * HD)
    width = HEADS * HD // N_TP
    total = jnp.zeros((RESP_DEV * RMAX, D), jnp.float32)
    for group in range(N_TP):
        partial_value = jnp.dot(attn[:, group * width:(group + 1) * width], w_out[group * width:(group + 1) * width], preferred_element_type=jnp.float32).astype(jnp.bfloat16)
        total = total + lax.optimization_barrier(partial_value).astype(jnp.float32)
    return total.astype(jnp.bfloat16).reshape(RESP_DEV, RMAX, D)

def reference(resp_rows, resp_len, resp_shard, group_prompt, prompt_kv, w_query, w_keyval, w_out):

    def one_group(items):
        rows, lengths, prompt = items
        cache = jnp.take(prompt_kv, prompt, axis=1)
        return group_output(rows, cache, lengths, w_query, w_keyval, w_out)
    outputs = lax.map(one_group, (resp_rows.reshape(N_SEQ, RESP_DEV, RMAX, D), resp_len.reshape(N_SEQ, RESP_DEV), group_prompt))
    table = resp_shard[:, 0].reshape(N_SEQ, RESP_DEV)
    same = table[:, :, None] == table[:, None, :]
    before = jnp.arange(RESP_DEV)[None, :] < jnp.arange(RESP_DEV)[:, None]
    rank = lax.optimization_barrier(jnp.sum((same & before[None, :, :]).astype(jnp.int32), -1))
    slot = table * SLOTS + jnp.arange(N_SEQ).astype(jnp.int32)[:, None] * CAP + rank
    attended = jnp.zeros((N_SEQ * SLOTS, RMAX, D), jnp.bfloat16)
    return attended.at[slot.reshape(-1).astype(jnp.int32)].set(outputs.reshape(RESPONSES, RMAX, D))
```

```python
import math

import jax
import jax.numpy as jnp
from jax import lax
from jax.sharding import PartitionSpec as P

HD = 128
PL = 256


ROPE_BASE = 1000000.0


def rope_tables(count, width, offset):
    places = (offset + jnp.arange(count)).astype(jnp.float32)
    freqs = ROPE_BASE ** (-(jnp.arange(width // 2).astype(jnp.float32) * 2.0 / width))
    angles = places[:, None] * freqs[None, :]
    return (jnp.cos(angles), jnp.sin(angles))


def rotate(values, cosine, sine):
    half = values.shape[-1] // 2
    first = values[..., :half]
    second = values[..., half:]
    cosine = cosine[:, None, :]
    sine = sine[:, None, :]
    return jnp.concatenate([first * cosine - second * sine, second * cosine + first * sine], -1)


def attend(queries, own_keys, own_values, cached_keys, cached_values, lengths):
    scale = 1.0 / math.sqrt(queries.shape[-1])
    prior = (
        jnp.einsum("stkrh,pkh->krstp", queries, cached_keys, preferred_element_type=jnp.float32)
        * scale
    )
    recent = (
        jnp.einsum("stkrh,sukh->krstu", queries, own_keys, preferred_element_type=jnp.float32)
        * scale
    )
    places = jnp.arange(queries.shape[1])
    causal = places[:, None] >= places[None, :]
    recent = jnp.where(causal, recent, -1e30)
    top = jnp.maximum(jnp.max(prior, -1), jnp.max(recent, -1))
    prior_exp = jnp.exp(prior - top[..., None])
    recent_exp = jnp.exp(recent - top[..., None])
    total = jnp.sum(prior_exp, -1) + jnp.sum(recent_exp, -1)
    prior_w = (prior_exp / total[..., None]).astype(jnp.bfloat16)
    recent_w = (recent_exp / total[..., None]).astype(jnp.bfloat16)
    mixed = jnp.einsum(
        "krstp,pkh->stkrh", prior_w, cached_values, preferred_element_type=jnp.float32
    )
    mixed = mixed + jnp.einsum(
        "krstu,sukh->stkrh", recent_w, own_values, preferred_element_type=jnp.float32
    )
    valid = places[None, :] < lengths[:, None]
    mixed = jnp.where(valid[:, :, None, None, None], mixed, 0.0)
    return mixed.astype(jnp.bfloat16).reshape(queries.shape[0], queries.shape[1], -1)


def choose(match, capacity):
    group_size = match.shape[1]
    rank = jnp.cumsum(match.astype(jnp.int32), axis=1) - 1
    picked = match[:, None, :] & (rank[:, None, :] == jnp.arange(capacity)[None, :, None])
    chosen = jnp.sum(jnp.where(picked, jnp.arange(group_size)[None, None, :], 0), -1)
    filled = jnp.any(picked, -1)
    return (chosen.reshape(-1), filled.reshape(-1))


def outgoing(resp_len, resp_shard, group_size):
    learners = lax.axis_size("seq")
    group = lax.axis_index("seq")
    capacity = (group_size + learners - 1) // learners
    own = lax.dynamic_slice_in_dim(resp_shard[:, 0], group * group_size, group_size, 0)
    pick, filled = choose(own[None, :] == jnp.arange(learners)[:, None], capacity)
    lengths = jnp.where(filled, resp_len[group * group_size + pick], 0)
    return pick, lengths


def per_device(resp_rows, resp_len, resp_shard, group_prompt, prompt_kv, w_query, w_keyval, w_out):
    group = lax.axis_index("seq")
    pick, lengths = outgoing(resp_len, resp_shard, resp_rows.shape[0])
    caches = lax.all_gather(prompt_kv, "seq", axis=1, tiled=True)
    cache = lax.dynamic_index_in_dim(caches, group_prompt[group], 1, keepdims=False)
    features = lax.all_gather(jnp.take(resp_rows, pick, axis=0), "tp", axis=2, tiled=True)
    slots, token_count, width = features.shape
    flat = features.reshape(slots * token_count, width)
    kv_local = w_keyval.shape[2] // HD
    q_local = w_query.shape[1] // HD
    ratio = q_local // kv_local
    cosine, sine = rope_tables(token_count, HD, PL)
    queries = jnp.dot(flat, w_query, preferred_element_type=jnp.float32).reshape(
        slots, token_count, q_local, HD
    )
    queries = (
        rotate(queries, cosine, sine)
        .astype(jnp.bfloat16)
        .reshape(slots, token_count, kv_local, ratio, HD)
    )
    keys = jnp.dot(flat, w_keyval[0], preferred_element_type=jnp.float32)
    keys = rotate(keys.reshape(slots, token_count, kv_local, HD), cosine, sine)
    keys = keys.astype(jnp.bfloat16)
    values = jnp.dot(flat, w_keyval[1], preferred_element_type=jnp.float32).astype(jnp.bfloat16)
    values = values.reshape(slots, token_count, kv_local, HD)
    cached_keys = cache[0].reshape(-1, kv_local, HD)
    cached_values = cache[1].reshape(-1, kv_local, HD)
    attn = attend(queries, keys, values, cached_keys, cached_values, lengths)
    partial_value = jnp.dot(
        attn.reshape(-1, q_local * HD), w_out, preferred_element_type=jnp.float32
    ).astype(jnp.bfloat16)
    summed = lax.psum_scatter(
        partial_value.reshape(slots, token_count, -1), "tp", scatter_dimension=2, tiled=True
    )
    return lax.all_to_all(summed, "seq", split_axis=0, concat_axis=0, tiled=True)


def solution(mesh):
    return jax.shard_map(
        per_device,
        mesh=mesh,
        in_specs=(
            P("seq", None, "tp"),
            P(),
            P(),
            P(),
            P(None, "seq", None, "tp"),
            P(None, "tp"),
            P(None, None, "tp"),
            P("tp", None),
        ),
        out_specs=P("seq", None, "tp"),
        check_vma=False,
    )
```

```python
import math

import jax
import jax.numpy as jnp
import numpy as np
from jax import lax
from jax.experimental import pallas as pl
from jax.experimental.pallas import tpu as pltpu
from jax.sharding import PartitionSpec as P

HD = 128
PL = 256
RMAX = 16


ROPE_BASE = 1000000.0


def rope_tables(count, width, offset):
    places = (offset + jnp.arange(count)).astype(jnp.float32)
    freqs = ROPE_BASE ** (-(jnp.arange(width // 2).astype(jnp.float32) * 2.0 / width))
    angles = places[:, None] * freqs[None, :]
    return (jnp.cos(angles), jnp.sin(angles))


def rotate(values, cosine, sine):
    half = values.shape[-1] // 2
    first = values[..., :half]
    second = values[..., half:]
    cosine = cosine[:, None, :]
    sine = sine[:, None, :]
    return jnp.concatenate([first * cosine - second * sine, second * cosine + first * sine], -1)


def attend(queries, own_keys, own_values, cached_keys, cached_values, lengths):
    scale = 1.0 / math.sqrt(queries.shape[-1])
    prior = (
        jnp.einsum("stkrh,pkh->krstp", queries, cached_keys, preferred_element_type=jnp.float32)
        * scale
    )
    recent = (
        jnp.einsum("stkrh,sukh->krstu", queries, own_keys, preferred_element_type=jnp.float32)
        * scale
    )
    places = jnp.arange(queries.shape[1])
    causal = places[:, None] >= places[None, :]
    recent = jnp.where(causal, recent, -1e30)
    top = jnp.maximum(jnp.max(prior, -1), jnp.max(recent, -1))
    prior_exp = jnp.exp(prior - top[..., None])
    recent_exp = jnp.exp(recent - top[..., None])
    total = jnp.sum(prior_exp, -1) + jnp.sum(recent_exp, -1)
    prior_w = (prior_exp / total[..., None]).astype(jnp.bfloat16)
    recent_w = (recent_exp / total[..., None]).astype(jnp.bfloat16)
    mixed = jnp.einsum(
        "krstp,pkh->stkrh", prior_w, cached_values, preferred_element_type=jnp.float32
    )
    mixed = mixed + jnp.einsum(
        "krstu,sukh->stkrh", recent_w, own_values, preferred_element_type=jnp.float32
    )
    valid = places[None, :] < lengths[:, None]
    mixed = jnp.where(valid[:, :, None, None, None], mixed, 0.0)
    return mixed.astype(jnp.bfloat16).reshape(queries.shape[0], queries.shape[1], -1)


def choose(match, capacity):
    group_size = match.shape[1]
    rank = jnp.cumsum(match.astype(jnp.int32), axis=1) - 1
    picked = match[:, None, :] & (rank[:, None, :] == jnp.arange(capacity)[None, :, None])
    chosen = jnp.sum(jnp.where(picked, jnp.arange(group_size)[None, None, :], 0), -1)
    filled = jnp.any(picked, -1)
    return (chosen.reshape(-1), filled.reshape(-1))


def outgoing(resp_len, resp_shard, group_size):
    learners = lax.axis_size("seq")
    group = lax.axis_index("seq")
    capacity = (group_size + learners - 1) // learners
    own = lax.dynamic_slice_in_dim(resp_shard[:, 0], group * group_size, group_size, 0)
    pick, filled = choose(own[None, :] == jnp.arange(learners)[:, None], capacity)
    lengths = jnp.where(filled, resp_len[group * group_size + pick], 0)
    return pick, lengths


def per_device(resp_rows, resp_len, resp_shard, group_prompt, prompt_kv, w_query, w_keyval, w_out):
    group = lax.axis_index("seq")
    pick, lengths = outgoing(resp_len, resp_shard, resp_rows.shape[0])
    caches = lax.all_gather(prompt_kv, "seq", axis=1, tiled=True)
    cache = lax.dynamic_index_in_dim(caches, group_prompt[group], 1, keepdims=False)
    features = lax.all_gather(jnp.take(resp_rows, pick, axis=0), "tp", axis=2, tiled=True)
    slots, token_count, width = features.shape
    flat = features.reshape(slots * token_count, width)
    kv_local = w_keyval.shape[2] // HD
    q_local = w_query.shape[1] // HD
    ratio = q_local // kv_local
    cosine, sine = rope_tables(token_count, HD, PL)
    queries = jnp.dot(flat, w_query, preferred_element_type=jnp.float32).reshape(
        slots, token_count, q_local, HD
    )
    queries = (
        rotate(queries, cosine, sine)
        .astype(jnp.bfloat16)
        .reshape(slots, token_count, kv_local, ratio, HD)
    )
    keys = jnp.dot(flat, w_keyval[0], preferred_element_type=jnp.float32)
    keys = rotate(keys.reshape(slots, token_count, kv_local, HD), cosine, sine)
    keys = keys.astype(jnp.bfloat16)
    values = jnp.dot(flat, w_keyval[1], preferred_element_type=jnp.float32).astype(jnp.bfloat16)
    values = values.reshape(slots, token_count, kv_local, HD)
    cached_keys = cache[0].reshape(-1, kv_local, HD)
    cached_values = cache[1].reshape(-1, kv_local, HD)
    attn = attend(queries, keys, values, cached_keys, cached_values, lengths)
    partial_value = jnp.dot(
        attn.reshape(-1, q_local * HD), w_out, preferred_element_type=jnp.float32
    ).astype(jnp.bfloat16)
    summed = lax.psum_scatter(
        partial_value.reshape(slots, token_count, -1), "tp", scatter_dimension=2, tiled=True
    )
    return lax.all_to_all(summed, "seq", split_axis=0, concat_axis=0, tiled=True)


MESH = pl.DeviceIdType.MESH
ORDER = (6, 7, 4, 5, 2, 3, 1, 0)
PIECES = 4


def fused_kernel(
    shard_ref, len_ref, prompt_ref, cos_ref, sin_ref, x_ref, kv_ref, wq_hbm, wkv_hbm, wo_hbm,
    out_ref,
    wq, wkv, wo, rows, acc, kbuf, vbuf, stage, landed, attn, queue, sibling, ahead, kept, across,
    done, arrived,
    load_sem, gather_send, gather_recv, line_send, line_recv, pair_send, pair_recv,
    sib_send, sib_recv, cross_send, cross_recv, out_send, out_recv,
):
    seq = lax.axis_index("seq")
    tp = lax.axis_index("tp")
    z, x = seq // 2, seq % 2
    y, c = tp // 2, tp % 2
    sib = y * 2 + (1 - c)
    opp = (1 - y) * 2 + c
    diag = (1 - y) * 2 + (1 - c)
    count, width = x_ref.shape
    f32, bf16 = jnp.float32, jnp.bfloat16

    def peer(m):
        zz = (z, z + 1 - 2 * (z % 2), z + 2 - 4 * (z // 2), 3 - z)[m // 2]
        return zz * 2 + (x, 1 - x)[m % 2]

    loads = [
        pltpu.make_async_copy(wq_hbm, wq, load_sem.at[0]),
        pltpu.make_async_copy(wkv_hbm, wkv, load_sem.at[1]),
        pltpu.make_async_copy(wo_hbm, wo, load_sem.at[2]),
    ]
    for load in loads:
        load.start()

    barrier = pltpu.get_barrier_semaphore()
    for m in range(1, 8):
        pl.semaphore_signal(barrier, inc=1, device_id=(peer(m), tp), device_id_type=MESH)
    for other in (sib, opp):
        pl.semaphore_signal(barrier, inc=1, device_id=(seq, other), device_id_type=MESH)
    pl.semaphore_wait(barrier, 9)

    def remote(src, dst, send, recv, device):
        return pltpu.make_async_remote_copy(
            src_ref=src, dst_ref=dst, send_sem=send, recv_sem=recv,
            device_id=device, device_id_type=MESH,
        )

    size = count // PIECES
    to_sib = remote(x_ref, rows.at[tp], gather_send.at[0], gather_recv.at[0], (seq, sib))
    to_opp, forward = [], []
    for i in range(PIECES):
        part = pl.ds(i * size, size)
        to_opp.append(
            remote(
                x_ref.at[part], rows.at[tp, part],
                gather_send.at[1 + i], gather_recv.at[1 + i], (seq, opp),
            )
        )
        forward.append(
            remote(
                rows.at[opp, part], rows.at[opp, part],
                gather_send.at[1 + PIECES + i], gather_recv.at[1 + PIECES + i], (seq, sib),
            )
        )

    bufs = (kbuf, vbuf)

    def hop(kind, way, step):
        block = z - step if way == 0 else z + step
        target = (z + 1 if way == 0 else z - 1) * 2 + x
        return remote(
            bufs[kind].at[block], bufs[kind].at[block],
            line_send.at[kind, way, step], line_recv.at[kind, block], (target, tp),
        )

    def can_send(way, step):
        return (z < 3) & (z >= step) if way == 0 else (z > 0) & (z + step <= 3)

    def has_source(way, step):
        return z >= step if way == 0 else z + step <= 3

    def launch(kind, step):
        for way in (0, 1):
            @pl.when(can_send(way, step))
            def _():
                hop(kind, way, step).start()

    def receive(kind, step):
        for way in (0, 1):
            @pl.when(has_source(way, step))
            def _():
                block = z - step if way == 0 else z + step
                remote(
                    bufs[kind].at[block], bufs[kind].at[block],
                    line_send.at[kind, way, 0], line_recv.at[kind, block], (seq, sib),
                ).wait_recv()

    kbuf[z] = kv_ref[0]
    vbuf[z] = kv_ref[1]
    for copy in to_opp:
        copy.start()
    launch(0, 0)
    launch(1, 0)
    to_sib.start()

    def advance(step):
        for kind in (0, 1):
            receive(kind, step)
            launch(kind, step)

    def relay(i):
        to_opp[i].wait_recv()
        forward[i].start()

    def project(owner, first):
        base = pl.multiple_of(owner * width, width)

        def add(n, value):
            if first:
                acc[n] = value
            else:
                acc[n] += value

        source = x_ref if first else rows.at[owner]

        def queries(n, carry):
            lanes = pl.ds(pl.multiple_of(n * 256, 256), 256)
            add(n, jnp.dot(source[...], wq[pl.ds(base, width), lanes], preferred_element_type=f32))
            return carry

        def keyval(n, carry):
            add(3 + n, jnp.dot(source[...], wkv[n, pl.ds(base, width), :], preferred_element_type=f32))
            return carry

        lax.fori_loop(0, 3, queries, 0)
        lax.fori_loop(0, 2, keyval, 0)

    advance(1)
    for i in range(PIECES // 2):
        relay(i)
    loads[0].wait()
    loads[1].wait()
    project(tp, True)
    to_sib.wait_recv()
    project(sib, False)
    advance(2)
    for i in range(PIECES // 2, PIECES - 1):
        relay(i)

    partner = peer(1)
    wanted = prompt_ref[partner]
    mine = prompt_ref[seq]

    def pair(kind):
        return remote(
            stage.at[kind], landed.at[kind], pair_send.at[kind], pair_recv.at[kind], (partner, tp)
        )

    receive(0, 3)
    stage[0] = kbuf[lax.shift_right_logical(wanted, 1)]
    pair(0).start()
    relay(PIECES - 1)
    project(opp, False)
    receive(1, 3)
    stage[1] = vbuf[lax.shift_right_logical(wanted, 1)]
    pair(1).start()
    for i in range(PIECES):
        forward[i].wait_recv()
    project(diag, False)

    lane = lax.broadcasted_iota(jnp.int32, (1, count), 1)
    token = lax.rem(lane, RMAX)
    owner_of = lax.div(lane, RMAX)
    group = count // RMAX
    shards = [shard_ref[seq * group + r] for r in range(group)]
    place = jnp.full((1, count), -1, jnp.int32)
    for r in range(group):
        rank = jnp.int32(0)
        for e in range(r):
            rank = rank + jnp.where(shards[e] == shards[r], 1, 0)
        slot = shards[r] * 2 + rank
        here = (owner_of == r) & (token < len_ref[seq * group + r])
        place = jnp.where(here, slot * RMAX + token, place)
    down = lax.broadcasted_iota(jnp.int32, (count, count), 0)
    across_i = lax.broadcasted_iota(jnp.int32, (count, count), 1)
    deal = jnp.where(down == place, 1.0, 0.0).astype(bf16)
    causal = (lax.div(down, RMAX) == lax.div(across_i, RMAX)) & (down >= across_i)

    cosine = cos_ref[...]
    sine = sin_ref[...]

    def turn(values):
        other = pltpu.roll(values, HD // 2, 1)
        shape = (count // RMAX, RMAX, HD)
        out = values.reshape(shape) * cosine[None] + other.reshape(shape) * sine[None]
        return out.reshape(count, HD).astype(bf16)

    local = lax.rem(mine, 2) == x
    scale = 1.0 / math.sqrt(HD)
    nt = (((1,), (1,)), ((), ()))
    pair(0).wait_recv()
    keys = jnp.where(local, kbuf[lax.shift_right_logical(mine, 1)], landed[0])
    pair(1).wait_recv()
    cached = jnp.where(local, vbuf[lax.shift_right_logical(mine, 1)], landed[1])
    for h in range(6):
        k = h // 3
        lanes = slice(k * HD, (k + 1) * HD)
        query = turn(acc[h // 2, :, (h % 2) * HD:(h % 2 + 1) * HD])
        if h % 3 == 0:
            own_key = turn(acc[3, :, lanes])
            own_value = acc[4, :, lanes].astype(bf16)
        prior = lax.dot_general(query, keys[:, lanes], nt, preferred_element_type=f32) * scale
        recent = lax.dot_general(query, own_key, nt, preferred_element_type=f32) * scale
        recent = jnp.where(causal, recent, -1e30)
        top = jnp.maximum(
            jnp.max(prior, -1, keepdims=True), jnp.max(recent, -1, keepdims=True)
        )
        prior = jnp.exp(prior - top)
        recent = jnp.exp(recent - top)
        share = 1.0 / (jnp.sum(prior, -1, keepdims=True) + jnp.sum(recent, -1, keepdims=True))
        mixed = jnp.dot(
            (prior * share).astype(bf16), cached[:, lanes], preferred_element_type=f32
        ) + jnp.dot((recent * share).astype(bf16), own_value, preferred_element_type=f32)
        mixed = jnp.dot(deal, mixed.astype(bf16), preferred_element_type=f32)
        attn[:, h * HD:(h + 1) * HD] = mixed.astype(bf16)

    loads[2].wait()

    def partial(owner, dst):
        def tile(n, carry):
            source = pl.ds(pl.multiple_of(owner * width + n * 256, 256), 256)
            lanes = pl.ds(pl.multiple_of(n * 256, 256), 256)
            dst[:, lanes] = jnp.dot(
                attn[...], wo[:, source], preferred_element_type=f32
            ).astype(bf16)
            return carry

        lax.fori_loop(0, width // 256, tile, 0)

    def swap(i):
        return remote(queue.at[i], sibling.at[i], sib_send.at[i], sib_recv.at[i], (seq, sib))

    span = count // 8

    def chunk(m):
        return pl.ds(pl.multiple_of(peer(m) * span, span), span)

    def cross(m):
        return remote(
            ahead.at[chunk(m)], across.at[chunk(m)], cross_send.at[m], cross_recv.at[m], (seq, opp)
        )

    def deliver(m):
        return remote(
            done.at[chunk(m)], arrived.at[seq], out_send.at[m], out_recv.at[m], (peer(m), tp)
        )

    def accept(m):
        return remote(
            done.at[chunk(m)], arrived.at[peer(m)], out_send.at[m], out_recv.at[m], (peer(m), tp)
        )

    partial(diag, queue.at[0])
    swap(0).start()
    partial(opp, ahead)
    swap(0).wait_recv()
    for m in ORDER:
        both = ahead[chunk(m)].astype(f32) + sibling[0, chunk(m)].astype(f32)
        ahead[chunk(m)] = both.astype(bf16)
        cross(m).start()
    partial(sib, queue.at[1])
    swap(1).start()
    partial(tp, kept)
    swap(1).wait_recv()
    for m in ORDER:
        cross(m).wait_recv()
        total = kept[chunk(m)].astype(f32) + sibling[1, chunk(m)].astype(f32)
        total = (total + across[chunk(m)].astype(f32)).astype(bf16)
        if m == 0:
            out_ref[chunk(0)] = total
        else:
            done[chunk(m)] = total
            deliver(m).start()
    for m in ORDER[:-1]:
        accept(m).wait_recv()
        out_ref[chunk(m)] = arrived[peer(m)]

    to_sib.wait_send()
    for i in range(PIECES):
        to_opp[i].wait_send()
        forward[i].wait_send()
    for kind in (0, 1):
        for step in range(3):
            for way in (0, 1):
                @pl.when(can_send(way, step))
                def _():
                    hop(kind, way, step).wait_send()
        pair(kind).wait_send()
        swap(kind).wait_send()
    for m in range(8):
        cross(m).wait_send()
    for m in range(1, 8):
        deliver(m).wait_send()


def fused_device(resp_rows, resp_len, resp_shard, group_prompt, prompt_kv, w_query, w_keyval, w_out):
    group, tokens, width = resp_rows.shape
    count = group * tokens
    angles = np.arange(PL, PL + tokens, dtype=np.float32)[:, None] * (
        ROPE_BASE ** (-np.arange(0, HD, 2, dtype=np.float64) / HD)
    ).astype(np.float32)
    cosine = np.concatenate([np.cos(angles), np.cos(angles)], -1).astype(np.float32)
    sine = np.concatenate([-np.sin(angles), np.sin(angles)], -1).astype(np.float32)
    bf16 = jnp.bfloat16
    block = (count, width)
    smem = pl.BlockSpec(memory_space=pltpu.SMEM)
    vmem = pl.BlockSpec(memory_space=pltpu.VMEM)
    hbm = pl.BlockSpec(memory_space=pl.ANY)
    dma = pltpu.SemaphoreType.DMA
    cache = (PL, w_keyval.shape[2])
    out = pl.pallas_call(
        fused_kernel,
        out_shape=jax.ShapeDtypeStruct(block, bf16),
        in_specs=[smem] * 3 + [vmem] * 4 + [hbm] * 3,
        out_specs=vmem,
        scratch_shapes=[
            pltpu.VMEM(w_query.shape, bf16),
            pltpu.VMEM(w_keyval.shape, bf16),
            pltpu.VMEM(w_out.shape, bf16),
            pltpu.VMEM((4,) + block, bf16),
            pltpu.VMEM((5, count, 256), jnp.float32),
            pltpu.VMEM((4,) + cache, bf16),
            pltpu.VMEM((4,) + cache, bf16),
            pltpu.VMEM((2,) + cache, bf16),
            pltpu.VMEM((2,) + cache, bf16),
            pltpu.VMEM((count, w_query.shape[1]), bf16),
            pltpu.VMEM((2,) + block, bf16),
            pltpu.VMEM((2,) + block, bf16),
            pltpu.VMEM(block, bf16),
            pltpu.VMEM(block, bf16),
            pltpu.VMEM(block, bf16),
            pltpu.VMEM(block, bf16),
            pltpu.VMEM((8, count // 8, width), bf16),
            dma((3,)),
            dma((1 + 2 * PIECES,)),
            dma((1 + 2 * PIECES,)),
            dma((2, 2, 3)),
            dma((2, 4)),
            dma((2,)),
            dma((2,)),
            dma((2,)),
            dma((2,)),
            dma((8,)),
            dma((8,)),
            dma((8,)),
            dma((8,)),
        ],
        compiler_params=pltpu.CompilerParams(
            collective_id=0, has_side_effects=True, vmem_limit_bytes=56 * 1024 * 1024
        ),
        cost_estimate=pl.CostEstimate(
            flops=6 * 10**9, bytes_accessed=23 * 10**6, transcendentals=10**6
        ),
    )(
        resp_shard[:, 0], resp_len, group_prompt, jnp.asarray(cosine), jnp.asarray(sine),
        resp_rows.reshape(block), prompt_kv[:, 0], w_query, w_keyval, w_out,
    )
    return out.reshape(group, tokens, width)


def fits(mesh):
    return mesh.shape["seq"] == 8 and mesh.shape["tp"] == 4


def solution(mesh):
    return jax.shard_map(
        fused_device if fits(mesh) else per_device,
        mesh=mesh,
        in_specs=(
            P("seq", None, "tp"),
            P(),
            P(),
            P(),
            P(None, "seq", None, "tp"),
            P(None, "tp"),
            P(None, None, "tp"),
            P("tp", None),
        ),
        out_specs=P("seq", None, "tp"),
        check_vma=False,
    )
```

```python
import math

import jax
import jax.numpy as jnp
import numpy as np
from jax import lax
from jax.experimental import pallas as pl
from jax.experimental.pallas import tpu as pltpu
from jax.sharding import PartitionSpec as P

HD = 128
PL = 256
RMAX = 16


ROPE_BASE = 1000000.0


def rope_tables(count, width, offset):
    places = (offset + jnp.arange(count)).astype(jnp.float32)
    freqs = ROPE_BASE ** (-(jnp.arange(width // 2).astype(jnp.float32) * 2.0 / width))
    angles = places[:, None] * freqs[None, :]
    return (jnp.cos(angles), jnp.sin(angles))


def rotate(values, cosine, sine):
    half = values.shape[-1] // 2
    first = values[..., :half]
    second = values[..., half:]
    cosine = cosine[:, None, :]
    sine = sine[:, None, :]
    return jnp.concatenate([first * cosine - second * sine, second * cosine + first * sine], -1)


def attend(queries, own_keys, own_values, cached_keys, cached_values, lengths):
    scale = 1.0 / math.sqrt(queries.shape[-1])
    prior = (
        jnp.einsum("stkrh,pkh->krstp", queries, cached_keys, preferred_element_type=jnp.float32)
        * scale
    )
    recent = (
        jnp.einsum("stkrh,sukh->krstu", queries, own_keys, preferred_element_type=jnp.float32)
        * scale
    )
    places = jnp.arange(queries.shape[1])
    causal = places[:, None] >= places[None, :]
    recent = jnp.where(causal, recent, -1e30)
    top = jnp.maximum(jnp.max(prior, -1), jnp.max(recent, -1))
    prior_exp = jnp.exp(prior - top[..., None])
    recent_exp = jnp.exp(recent - top[..., None])
    total = jnp.sum(prior_exp, -1) + jnp.sum(recent_exp, -1)
    prior_w = (prior_exp / total[..., None]).astype(jnp.bfloat16)
    recent_w = (recent_exp / total[..., None]).astype(jnp.bfloat16)
    mixed = jnp.einsum(
        "krstp,pkh->stkrh", prior_w, cached_values, preferred_element_type=jnp.float32
    )
    mixed = mixed + jnp.einsum(
        "krstu,sukh->stkrh", recent_w, own_values, preferred_element_type=jnp.float32
    )
    valid = places[None, :] < lengths[:, None]
    mixed = jnp.where(valid[:, :, None, None, None], mixed, 0.0)
    return mixed.astype(jnp.bfloat16).reshape(queries.shape[0], queries.shape[1], -1)


def choose(match, capacity):
    group_size = match.shape[1]
    rank = jnp.cumsum(match.astype(jnp.int32), axis=1) - 1
    picked = match[:, None, :] & (rank[:, None, :] == jnp.arange(capacity)[None, :, None])
    chosen = jnp.sum(jnp.where(picked, jnp.arange(group_size)[None, None, :], 0), -1)
    filled = jnp.any(picked, -1)
    return (chosen.reshape(-1), filled.reshape(-1))


def outgoing(resp_len, resp_shard, group_size):
    learners = lax.axis_size("seq")
    group = lax.axis_index("seq")
    capacity = (group_size + learners - 1) // learners
    own = lax.dynamic_slice_in_dim(resp_shard[:, 0], group * group_size, group_size, 0)
    pick, filled = choose(own[None, :] == jnp.arange(learners)[:, None], capacity)
    lengths = jnp.where(filled, resp_len[group * group_size + pick], 0)
    return pick, lengths


def per_device(resp_rows, resp_len, resp_shard, group_prompt, prompt_kv, w_query, w_keyval, w_out):
    group = lax.axis_index("seq")
    pick, lengths = outgoing(resp_len, resp_shard, resp_rows.shape[0])
    caches = lax.all_gather(prompt_kv, "seq", axis=1, tiled=True)
    cache = lax.dynamic_index_in_dim(caches, group_prompt[group], 1, keepdims=False)
    features = lax.all_gather(jnp.take(resp_rows, pick, axis=0), "tp", axis=2, tiled=True)
    slots, token_count, width = features.shape
    flat = features.reshape(slots * token_count, width)
    kv_local = w_keyval.shape[2] // HD
    q_local = w_query.shape[1] // HD
    ratio = q_local // kv_local
    cosine, sine = rope_tables(token_count, HD, PL)
    queries = jnp.dot(flat, w_query, preferred_element_type=jnp.float32).reshape(
        slots, token_count, q_local, HD
    )
    queries = (
        rotate(queries, cosine, sine)
        .astype(jnp.bfloat16)
        .reshape(slots, token_count, kv_local, ratio, HD)
    )
    keys = jnp.dot(flat, w_keyval[0], preferred_element_type=jnp.float32)
    keys = rotate(keys.reshape(slots, token_count, kv_local, HD), cosine, sine)
    keys = keys.astype(jnp.bfloat16)
    values = jnp.dot(flat, w_keyval[1], preferred_element_type=jnp.float32).astype(jnp.bfloat16)
    values = values.reshape(slots, token_count, kv_local, HD)
    cached_keys = cache[0].reshape(-1, kv_local, HD)
    cached_values = cache[1].reshape(-1, kv_local, HD)
    attn = attend(queries, keys, values, cached_keys, cached_values, lengths)
    partial_value = jnp.dot(
        attn.reshape(-1, q_local * HD), w_out, preferred_element_type=jnp.float32
    ).astype(jnp.bfloat16)
    summed = lax.psum_scatter(
        partial_value.reshape(slots, token_count, -1), "tp", scatter_dimension=2, tiled=True
    )
    return lax.all_to_all(summed, "seq", split_axis=0, concat_axis=0, tiled=True)


MESH = pl.DeviceIdType.MESH
ORDER = (6, 7, 4, 5, 2, 3, 1, 0)
PIECES = 4


def fused_kernel(
    shard_ref, len_ref, prompt_ref, cos_hbm, sin_hbm, x_hbm, kv_hbm, wq_hbm, wkv_hbm, wo_hbm,
    out_ref,
    wq, wkv, wo, rows, acc, cos_ref, sin_ref, buf0, buf1, buf2, buf3, stage, landed, dealt, valid,
    attn, queue, sibling, ahead, kept, across, done,
    load_sem, gather_send, gather_recv, line_send, line_recv, pair_send, pair_recv,
    sib_send, sib_recv, cross_send, cross_recv, out_send, out_recv,
):
    seq = lax.axis_index("seq")
    tp = lax.axis_index("tp")
    z, x = seq // 2, seq % 2
    y, c = tp // 2, tp % 2
    sib = y * 2 + (1 - c)
    opp = (1 - y) * 2 + c
    diag = (1 - y) * 2 + (1 - c)
    count, width = x_hbm.shape
    f32, bf16 = jnp.float32, jnp.bfloat16
    bufs = (buf0, buf1, buf2, buf3)
    part_len = PL // 2

    def peer(m):
        zz = (z, z + 1 - 2 * (z % 2), z + 2 - 4 * (z // 2), 3 - z)[m // 2]
        return zz * 2 + (x, 1 - x)[m % 2]

    def local(src, dst, i):
        return pltpu.make_async_copy(src, dst, load_sem.at[i])

    x_load = local(x_hbm, rows.at[tp], 0)
    kv_loads = [
        local(kv_hbm.at[k // 2, pl.ds((k % 2) * part_len, part_len)], bufs[k].at[z], 1 + k)
        for k in range(4)
    ]
    tables = [local(cos_hbm, cos_ref, 5), local(sin_hbm, sin_ref, 6)]
    loads = [local(wq_hbm, wq, 7), local(wkv_hbm, wkv, 8), local(wo_hbm, wo, 9)]
    for load in [x_load] + kv_loads + tables + loads:
        load.start()

    barrier = pltpu.get_barrier_semaphore()
    for m in range(1, 8):
        pl.semaphore_signal(barrier, inc=1, device_id=(peer(m), tp), device_id_type=MESH)
    for other in (sib, opp):
        pl.semaphore_signal(barrier, inc=1, device_id=(seq, other), device_id_type=MESH)
    pl.semaphore_wait(barrier, 9)

    def remote(src, dst, send, recv, device):
        return pltpu.make_async_remote_copy(
            src_ref=src, dst_ref=dst, send_sem=send, recv_sem=recv,
            device_id=device, device_id_type=MESH,
        )

    size = count // PIECES
    to_sib = remote(rows.at[tp], rows.at[tp], gather_send.at[0], gather_recv.at[0], (seq, sib))
    to_opp, forward = [], []
    for i in range(PIECES):
        part = pl.ds(i * size, size)
        to_opp.append(
            remote(
                rows.at[tp, part], rows.at[tp, part],
                gather_send.at[1 + i], gather_recv.at[1 + i], (seq, opp),
            )
        )
        forward.append(
            remote(
                rows.at[opp, part], rows.at[opp, part],
                gather_send.at[1 + PIECES + i], gather_recv.at[1 + PIECES + i], (seq, sib),
            )
        )

    def hop(kind, way, step):
        block = z - step if way == 0 else z + step
        target = (z + 1 if way == 0 else z - 1) * 2 + x
        return remote(
            bufs[kind].at[block], bufs[kind].at[block],
            line_send.at[kind, way, step], line_recv.at[kind, block], (target, tp),
        )

    def can_send(way, step):
        return (z < 3) & (z >= step) if way == 0 else (z > 0) & (z + step <= 3)

    def has_source(way, step):
        return z >= step if way == 0 else z + step <= 3

    def launch(kind, step):
        for way in (0, 1):
            @pl.when(can_send(way, step))
            def _():
                hop(kind, way, step).start()

    def receive(kind, step):
        for way in (0, 1):
            @pl.when(has_source(way, step))
            def _():
                block = z - step if way == 0 else z + step
                remote(
                    bufs[kind].at[block], bufs[kind].at[block],
                    line_send.at[kind, way, 0], line_recv.at[kind, block], (seq, sib),
                ).wait_recv()

    x_load.wait()
    for copy in to_opp:
        copy.start()
    for kind in range(4):
        kv_loads[kind].wait()
        launch(kind, 0)
    to_sib.start()

    def advance(step, kinds):
        for kind in kinds:
            receive(kind, step)
            launch(kind, step)

    def relay(i):
        to_opp[i].wait_recv()
        forward[i].start()

    def project(owner, first):
        base = pl.multiple_of(owner * width, width)

        def add(n, value):
            if first:
                acc[n] = value
            else:
                acc[n] += value

        source = rows.at[owner]

        def queries(n, carry):
            lanes = pl.ds(pl.multiple_of(n * 256, 256), 256)
            add(n, jnp.dot(source[...], wq[pl.ds(base, width), lanes], preferred_element_type=f32))
            return carry

        def keyval(n, carry):
            add(3 + n, jnp.dot(source[...], wkv[n, pl.ds(base, width), :], preferred_element_type=f32))
            return carry

        lax.fori_loop(0, 3, queries, 0)
        lax.fori_loop(0, 2, keyval, 0)

    partner = peer(1)
    wanted = lax.shift_right_logical(prompt_ref[partner], 1)

    def pair(kind):
        return remote(
            stage.at[kind], landed.at[kind], pair_send.at[kind], pair_recv.at[kind], (partner, tp)
        )

    def hand_over(kind):
        receive(kind, 3)
        stage[kind] = bufs[kind][wanted]
        pair(kind).start()

    advance(1, (0, 1, 2, 3))
    loads[0].wait()
    loads[1].wait()
    project(tp, True)
    relay(0)
    advance(2, (0, 1))
    relay(1)
    to_sib.wait_recv()
    project(sib, False)
    advance(2, (2, 3))
    relay(2)
    hand_over(0)
    hand_over(1)

    lane = lax.broadcasted_iota(jnp.int32, (1, count), 1)
    token = lax.rem(lane, RMAX)
    owner_of = lax.div(lane, RMAX)
    group = count // RMAX
    shards = [shard_ref[seq * group + r] for r in range(group)]
    place = jnp.full((1, count), -1, jnp.int32)
    for r in range(group):
        rank = jnp.int32(0)
        for e in range(r):
            rank = rank + jnp.where(shards[e] == shards[r], 1, 0)
        slot = shards[r] * 2 + rank
        here = (owner_of == r) & (token < len_ref[seq * group + r])
        place = jnp.where(here, slot * RMAX + token, place)
    down = lax.broadcasted_iota(jnp.int32, (count, count), 0)
    deal = jnp.where(down == place, 1.0, 0.0).astype(bf16)
    valid[...] = jnp.broadcast_to(
        jnp.sum(deal.astype(f32), -1, keepdims=True), valid.shape
    )
    half = count // 2
    row = lax.broadcasted_iota(jnp.int32, (half, half), 0)
    col = lax.broadcasted_iota(jnp.int32, (half, half), 1)
    causal = (lax.div(row, RMAX) == lax.div(col, RMAX)) & (row >= col)

    relay(PIECES - 1)
    project(opp, False)
    hand_over(2)
    hand_over(3)
    for i in range(PIECES):
        forward[i].wait_recv()
    project(diag, False)

    for table in tables:
        table.wait()
    cosine = cos_ref[...]
    sine = sin_ref[...]

    def turn(values):
        other = pltpu.roll(values, HD // 2, 1)
        shape = (count // RMAX, RMAX, HD)
        out = values.reshape(shape) * cosine[None] + other.reshape(shape) * sine[None]
        return out.reshape(count, HD).astype(bf16)

    for n in range(5):
        if n < 4:
            tile = jnp.concatenate([turn(acc[n, :, :HD]), turn(acc[n, :, HD:])], -1)
        else:
            tile = acc[n].astype(bf16)
        dealt[n] = jnp.dot(deal, tile, preferred_element_type=f32).astype(bf16)

    mine = prompt_ref[seq]
    here_too = lax.rem(mine, 2) == x
    scale = 1.0 / math.sqrt(HD)
    nt = (((1,), (1,)), ((), ()))

    def fetch(kind):
        pair(kind).wait_recv()
        return jnp.where(here_too, bufs[kind][lax.shift_right_logical(mine, 1)], landed[kind])

    for kind in range(4):
        landed[kind] = fetch(kind)

    def attend_rows(base):
        span_rows = pl.ds(base, half)
        mask = valid[span_rows, :1]
        for h in range(6):
            k = h // 3
            lanes = slice(k * HD, (k + 1) * HD)
            query = dealt[h // 2, span_rows, (h % 2) * HD:(h % 2 + 1) * HD]
            own_key = dealt[3, span_rows, lanes]
            own_value = dealt[4, span_rows, lanes]
            first = lax.dot_general(query, landed[0, :, lanes], nt, preferred_element_type=f32)
            second = lax.dot_general(query, landed[1, :, lanes], nt, preferred_element_type=f32)
            recent = lax.dot_general(query, own_key, nt, preferred_element_type=f32) * scale
            first, second = first * scale, second * scale
            recent = jnp.where(causal, recent, -1e30)
            top = jnp.max(
                jnp.maximum(jnp.maximum(first, second), recent), -1, keepdims=True
            )
            first, second = jnp.exp(first - top), jnp.exp(second - top)
            recent = jnp.exp(recent - top)
            share = mask / jnp.sum(first + second + recent, -1, keepdims=True)
            mixed = (
                jnp.dot((first * share).astype(bf16), landed[2, :, lanes],
                        preferred_element_type=f32)
                + jnp.dot((second * share).astype(bf16), landed[3, :, lanes],
                          preferred_element_type=f32)
                + jnp.dot((recent * share).astype(bf16), own_value, preferred_element_type=f32)
            )
            attn[span_rows, h * HD:(h + 1) * HD] = mixed.astype(bf16)

    def partial(owner, dst, base):
        span_rows = pl.ds(base, half)

        def tile(n, carry):
            source = pl.ds(pl.multiple_of(owner * width + n * 256, 256), 256)
            lanes = pl.ds(pl.multiple_of(n * 256, 256), 256)
            dst[span_rows, lanes] = jnp.dot(
                attn[span_rows], wo[:, source], preferred_element_type=f32
            ).astype(bf16)
            return carry

        lax.fori_loop(0, width // 256, tile, 0)

    def swap(i, side):
        span_rows = pl.ds(bases[side], half)
        return remote(
            queue.at[i, span_rows], sibling.at[i, span_rows],
            sib_send.at[i, side], sib_recv.at[i, side], (seq, sib),
        )

    span = count // 8

    def chunk(m):
        return pl.ds(pl.multiple_of(peer(m) * span, span), span)

    def cross(m):
        return remote(
            ahead.at[chunk(m)], across.at[chunk(m)], cross_send.at[m], cross_recv.at[m], (seq, opp)
        )

    home = pl.ds(pl.multiple_of(seq * span, span), span)

    def deliver(m):
        return remote(
            done.at[chunk(m)], out_ref.at[home], out_send.at[m], out_recv.at[m], (peer(m), tp)
        )

    def accept(m):
        return remote(
            done.at[chunk(m)], out_ref.at[chunk(m)], out_send.at[m], out_recv.at[m], (peer(m), tp)
        )

    stay = pltpu.make_async_copy(done.at[home], out_ref.at[home], out_send.at[0])

    def pass_on(m):
        both = ahead[chunk(m)].astype(f32) + sibling[0, chunk(m)].astype(f32)
        ahead[chunk(m)] = both.astype(bf16)
        cross(m).start()

    def finish(m):
        cross(m).wait_recv()
        total = kept[chunk(m)].astype(f32) + sibling[1, chunk(m)].astype(f32)
        done[chunk(m)] = (total + across[chunk(m)].astype(f32)).astype(bf16)
        if m == 0:
            stay.start()
        else:
            deliver(m).start()

    bases = (
        pl.multiple_of((1 - z // 2) * half, half),
        pl.multiple_of((z // 2) * half, half),
    )
    loads[2].wait()
    attend_rows(bases[0])
    partial(diag, queue.at[0], bases[0])
    swap(0, 0).start()
    partial(opp, ahead, bases[0])
    partial(sib, queue.at[1], bases[0])
    swap(1, 0).start()
    swap(0, 0).wait_recv()
    for m in ORDER[:4]:
        pass_on(m)
    partial(tp, kept, bases[0])
    attend_rows(bases[1])
    swap(1, 0).wait_recv()
    finish(ORDER[0])
    partial(diag, queue.at[0], bases[1])
    swap(0, 1).start()
    partial(opp, ahead, bases[1])
    partial(sib, queue.at[1], bases[1])
    swap(1, 1).start()
    swap(0, 1).wait_recv()
    for m in ORDER[4:]:
        pass_on(m)
    finish(ORDER[1])
    partial(tp, kept, bases[1])
    finish(ORDER[2])
    finish(ORDER[3])
    swap(1, 1).wait_recv()
    for m in ORDER[4:]:
        finish(m)
    for m in ORDER[:-1]:
        accept(m).wait_recv()
    stay.wait()

    to_sib.wait_send()
    for i in range(PIECES):
        to_opp[i].wait_send()
        forward[i].wait_send()
    for kind in range(4):
        for step in range(3):
            for way in (0, 1):
                @pl.when(can_send(way, step))
                def _():
                    hop(kind, way, step).wait_send()
        pair(kind).wait_send()
    for i in (0, 1):
        for side in (0, 1):
            swap(i, side).wait_send()
    for m in range(8):
        cross(m).wait_send()
    for m in range(1, 8):
        deliver(m).wait_send()


def fused_device(resp_rows, resp_len, resp_shard, group_prompt, prompt_kv, w_query, w_keyval, w_out):
    group, tokens, width = resp_rows.shape
    count = group * tokens
    angles = np.arange(PL, PL + tokens, dtype=np.float32)[:, None] * (
        ROPE_BASE ** (-np.arange(0, HD, 2, dtype=np.float64) / HD)
    ).astype(np.float32)
    cosine = np.concatenate([np.cos(angles), np.cos(angles)], -1).astype(np.float32)
    sine = np.concatenate([-np.sin(angles), np.sin(angles)], -1).astype(np.float32)
    bf16 = jnp.bfloat16
    block = (count, width)
    smem = pl.BlockSpec(memory_space=pltpu.SMEM)
    hbm = pl.BlockSpec(memory_space=pl.ANY)
    dma = pltpu.SemaphoreType.DMA
    cache = (PL // 2, w_keyval.shape[2])
    out = pl.pallas_call(
        fused_kernel,
        out_shape=jax.ShapeDtypeStruct(block, bf16),
        in_specs=[smem] * 3 + [hbm] * 7,
        out_specs=hbm,
        scratch_shapes=[
            pltpu.VMEM(w_query.shape, bf16),
            pltpu.VMEM(w_keyval.shape, bf16),
            pltpu.VMEM(w_out.shape, bf16),
            pltpu.VMEM((4,) + block, bf16),
            pltpu.VMEM((5, count, 256), jnp.float32),
            pltpu.VMEM((tokens, HD), jnp.float32),
            pltpu.VMEM((tokens, HD), jnp.float32),
            pltpu.VMEM((4,) + cache, bf16),
            pltpu.VMEM((4,) + cache, bf16),
            pltpu.VMEM((4,) + cache, bf16),
            pltpu.VMEM((4,) + cache, bf16),
            pltpu.VMEM((4,) + cache, bf16),
            pltpu.VMEM((4,) + cache, bf16),
            pltpu.VMEM((5, count, 256), bf16),
            pltpu.VMEM((count, HD), jnp.float32),
            pltpu.VMEM((count, w_query.shape[1]), bf16),
            pltpu.VMEM((2,) + block, bf16),
            pltpu.VMEM((2,) + block, bf16),
            pltpu.VMEM(block, bf16),
            pltpu.VMEM(block, bf16),
            pltpu.VMEM(block, bf16),
            pltpu.VMEM(block, bf16),
            dma((10,)),
            dma((1 + 2 * PIECES,)),
            dma((1 + 2 * PIECES,)),
            dma((4, 2, 3)),
            dma((4, 4)),
            dma((4,)),
            dma((4,)),
            dma((2, 2)),
            dma((2, 2)),
            dma((8,)),
            dma((8,)),
            dma((8,)),
            dma((8,)),
        ],
        compiler_params=pltpu.CompilerParams(
            collective_id=0, has_side_effects=True, vmem_limit_bytes=56 * 1024 * 1024
        ),
        cost_estimate=pl.CostEstimate(
            flops=6 * 10**9, bytes_accessed=23 * 10**6, transcendentals=10**6
        ),
    )(
        resp_shard[:, 0], resp_len, group_prompt, jnp.asarray(cosine), jnp.asarray(sine),
        resp_rows.reshape(block), prompt_kv[:, 0], w_query, w_keyval, w_out,
    )
    return out.reshape(group, tokens, width)


def fits(mesh):
    return mesh.shape["seq"] == 8 and mesh.shape["tp"] == 4


def solution(mesh):
    return jax.shard_map(
        fused_device if fits(mesh) else per_device,
        mesh=mesh,
        in_specs=(
            P("seq", None, "tp"),
            P(),
            P(),
            P(),
            P(None, "seq", None, "tp"),
            P(None, "tp"),
            P(None, None, "tp"),
            P("tp", None),
        ),
        out_specs=P("seq", None, "tp"),
        check_vma=False,
    )
```

```python
import math

import jax
import jax.numpy as jnp
import numpy as np
from jax import lax
from jax.experimental import pallas as pl
from jax.experimental.pallas import tpu as pltpu
from jax.sharding import PartitionSpec as P

HD = 128
PL = 256
RMAX = 16


ROPE_BASE = 1000000.0


def rope_tables(count, width, offset):
    places = (offset + jnp.arange(count)).astype(jnp.float32)
    freqs = ROPE_BASE ** (-(jnp.arange(width // 2).astype(jnp.float32) * 2.0 / width))
    angles = places[:, None] * freqs[None, :]
    return (jnp.cos(angles), jnp.sin(angles))


def rotate(values, cosine, sine):
    half = values.shape[-1] // 2
    first = values[..., :half]
    second = values[..., half:]
    cosine = cosine[:, None, :]
    sine = sine[:, None, :]
    return jnp.concatenate([first * cosine - second * sine, second * cosine + first * sine], -1)


def attend(queries, own_keys, own_values, cached_keys, cached_values, lengths):
    scale = 1.0 / math.sqrt(queries.shape[-1])
    prior = (
        jnp.einsum("stkrh,pkh->krstp", queries, cached_keys, preferred_element_type=jnp.float32)
        * scale
    )
    recent = (
        jnp.einsum("stkrh,sukh->krstu", queries, own_keys, preferred_element_type=jnp.float32)
        * scale
    )
    places = jnp.arange(queries.shape[1])
    causal = places[:, None] >= places[None, :]
    recent = jnp.where(causal, recent, -1e30)
    top = jnp.maximum(jnp.max(prior, -1), jnp.max(recent, -1))
    prior_exp = jnp.exp(prior - top[..., None])
    recent_exp = jnp.exp(recent - top[..., None])
    total = jnp.sum(prior_exp, -1) + jnp.sum(recent_exp, -1)
    prior_w = (prior_exp / total[..., None]).astype(jnp.bfloat16)
    recent_w = (recent_exp / total[..., None]).astype(jnp.bfloat16)
    mixed = jnp.einsum(
        "krstp,pkh->stkrh", prior_w, cached_values, preferred_element_type=jnp.float32
    )
    mixed = mixed + jnp.einsum(
        "krstu,sukh->stkrh", recent_w, own_values, preferred_element_type=jnp.float32
    )
    valid = places[None, :] < lengths[:, None]
    mixed = jnp.where(valid[:, :, None, None, None], mixed, 0.0)
    return mixed.astype(jnp.bfloat16).reshape(queries.shape[0], queries.shape[1], -1)


def choose(match, capacity):
    group_size = match.shape[1]
    rank = jnp.cumsum(match.astype(jnp.int32), axis=1) - 1
    picked = match[:, None, :] & (rank[:, None, :] == jnp.arange(capacity)[None, :, None])
    chosen = jnp.sum(jnp.where(picked, jnp.arange(group_size)[None, None, :], 0), -1)
    filled = jnp.any(picked, -1)
    return (chosen.reshape(-1), filled.reshape(-1))


def outgoing(resp_len, resp_shard, group_size):
    learners = lax.axis_size("seq")
    group = lax.axis_index("seq")
    capacity = (group_size + learners - 1) // learners
    own = lax.dynamic_slice_in_dim(resp_shard[:, 0], group * group_size, group_size, 0)
    pick, filled = choose(own[None, :] == jnp.arange(learners)[:, None], capacity)
    lengths = jnp.where(filled, resp_len[group * group_size + pick], 0)
    return pick, lengths


def per_device(resp_rows, resp_len, resp_shard, group_prompt, prompt_kv, w_query, w_keyval, w_out):
    group = lax.axis_index("seq")
    pick, lengths = outgoing(resp_len, resp_shard, resp_rows.shape[0])
    caches = lax.all_gather(prompt_kv, "seq", axis=1, tiled=True)
    cache = lax.dynamic_index_in_dim(caches, group_prompt[group], 1, keepdims=False)
    features = lax.all_gather(jnp.take(resp_rows, pick, axis=0), "tp", axis=2, tiled=True)
    slots, token_count, width = features.shape
    flat = features.reshape(slots * token_count, width)
    kv_local = w_keyval.shape[2] // HD
    q_local = w_query.shape[1] // HD
    ratio = q_local // kv_local
    cosine, sine = rope_tables(token_count, HD, PL)
    queries = jnp.dot(flat, w_query, preferred_element_type=jnp.float32).reshape(
        slots, token_count, q_local, HD
    )
    queries = (
        rotate(queries, cosine, sine)
        .astype(jnp.bfloat16)
        .reshape(slots, token_count, kv_local, ratio, HD)
    )
    keys = jnp.dot(flat, w_keyval[0], preferred_element_type=jnp.float32)
    keys = rotate(keys.reshape(slots, token_count, kv_local, HD), cosine, sine)
    keys = keys.astype(jnp.bfloat16)
    values = jnp.dot(flat, w_keyval[1], preferred_element_type=jnp.float32).astype(jnp.bfloat16)
    values = values.reshape(slots, token_count, kv_local, HD)
    cached_keys = cache[0].reshape(-1, kv_local, HD)
    cached_values = cache[1].reshape(-1, kv_local, HD)
    attn = attend(queries, keys, values, cached_keys, cached_values, lengths)
    partial_value = jnp.dot(
        attn.reshape(-1, q_local * HD), w_out, preferred_element_type=jnp.float32
    ).astype(jnp.bfloat16)
    summed = lax.psum_scatter(
        partial_value.reshape(slots, token_count, -1), "tp", scatter_dimension=2, tiled=True
    )
    return lax.all_to_all(summed, "seq", split_axis=0, concat_axis=0, tiled=True)


MESH = pl.DeviceIdType.MESH
ORDER = (6, 7, 4, 5, 2, 3, 1, 0)
PIECES = 5


def fused_kernel(
    shard_ref, len_ref, prompt_ref, cos_hbm, sin_hbm, x_hbm, kv_hbm, wq_hbm, wkv_hbm, wo_hbm,
    out_ref,
    wq, wkv, wo, rows, acc, cos_ref, sin_ref, buf0, buf1, buf2, buf3, stage, landed, dealt, valid,
    attn, queue, sibling, ahead, kept, across, done,
    load_sem, gather_send, gather_recv, line_send, line_recv, pair_send, pair_recv,
    sib_send, sib_recv, cross_send, cross_recv, out_send, out_recv,
):
    seq = lax.axis_index("seq")
    tp = lax.axis_index("tp")
    z, x = seq // 2, seq % 2
    y, c = tp // 2, tp % 2
    sib = y * 2 + (1 - c)
    opp = (1 - y) * 2 + c
    diag = (1 - y) * 2 + (1 - c)
    count, width = x_hbm.shape
    f32, bf16 = jnp.float32, jnp.bfloat16
    bufs = (buf0, buf1, buf2, buf3)
    part_len = PL // 2

    def peer(m):
        zz = (z, z + 1 - 2 * (z % 2), z + 2 - 4 * (z // 2), 3 - z)[m // 2]
        return zz * 2 + (x, 1 - x)[m % 2]

    def local(src, dst, i):
        return pltpu.make_async_copy(src, dst, load_sem.at[i])

    x_load = local(x_hbm, rows.at[tp], 0)
    kv_loads = [
        local(kv_hbm.at[k // 2, pl.ds((k % 2) * part_len, part_len)], bufs[k].at[z], 1 + k)
        for k in range(4)
    ]
    tables = [local(cos_hbm, cos_ref, 5), local(sin_hbm, sin_ref, 6)]
    blocks = []
    for i, owner in enumerate((tp, sib, opp, diag)):
        part = pl.ds(pl.multiple_of(owner * width, width), width)
        blocks.append((
            local(wq_hbm.at[part], wq.at[part], 7 + 2 * i),
            local(wkv_hbm.at[:, part], wkv.at[:, part], 8 + 2 * i),
        ))
    wo_load = local(wo_hbm, wo, 15)
    for load in [x_load] + kv_loads + tables:
        load.start()
    for block in blocks:
        for load in block:
            load.start()
    wo_load.start()

    barrier = pltpu.get_barrier_semaphore()
    for m in range(1, 8):
        pl.semaphore_signal(barrier, inc=1, device_id=(peer(m), tp), device_id_type=MESH)
    for other in (sib, opp):
        pl.semaphore_signal(barrier, inc=1, device_id=(seq, other), device_id_type=MESH)
    pl.semaphore_wait(barrier, 9)

    def remote(src, dst, send, recv, device):
        return pltpu.make_async_remote_copy(
            src_ref=src, dst_ref=dst, send_sem=send, recv_sem=recv,
            device_id=device, device_id_type=MESH,
        )

    size = width // PIECES
    to_sib = remote(rows.at[tp], rows.at[tp], gather_send.at[0], gather_recv.at[0], (seq, sib))
    to_opp, forward = [], []
    for i in range(PIECES):
        part = pl.ds(i * size, size)
        to_opp.append(
            remote(
                rows.at[tp, :, part], rows.at[tp, :, part],
                gather_send.at[1 + i], gather_recv.at[1 + i], (seq, opp),
            )
        )
        forward.append(
            remote(
                rows.at[opp, :, part], rows.at[opp, :, part],
                gather_send.at[1 + PIECES + i], gather_recv.at[1 + PIECES + i], (seq, sib),
            )
        )

    def hop(kind, way, step):
        block = z - step if way == 0 else z + step
        target = (z + 1 if way == 0 else z - 1) * 2 + x
        return remote(
            bufs[kind].at[block], bufs[kind].at[block],
            line_send.at[kind, way, step], line_recv.at[kind, block], (target, tp),
        )

    def can_send(way, step):
        return (z < 3) & (z >= step) if way == 0 else (z > 0) & (z + step <= 3)

    def has_source(way, step):
        return z >= step if way == 0 else z + step <= 3

    def launch(kind, step):
        for way in (0, 1):
            @pl.when(can_send(way, step))
            def _():
                hop(kind, way, step).start()

    def receive(kind, step):
        for way in (0, 1):
            @pl.when(has_source(way, step))
            def _():
                block = z - step if way == 0 else z + step
                remote(
                    bufs[kind].at[block], bufs[kind].at[block],
                    line_send.at[kind, way, 0], line_recv.at[kind, block], (seq, sib),
                ).wait_recv()

    x_load.wait()
    for copy in to_opp:
        copy.start()
    for kind in range(4):
        kv_loads[kind].wait()
        launch(kind, 0)
    to_sib.start()

    def advance(step, kinds):
        for kind in kinds:
            receive(kind, step)
            launch(kind, step)

    def relay(i):
        to_opp[i].wait_recv()
        forward[i].start()

    def project(owner, start, depth, first):
        base = pl.multiple_of(owner * width + start, 256)
        source = rows[owner, :, start:start + depth]
        for n in range(5):
            if n < 3:
                weight = wq[pl.ds(base, depth), n * 256:(n + 1) * 256]
            else:
                weight = wkv[n - 3, pl.ds(base, depth), :]
            value = jnp.dot(source, weight, preferred_element_type=f32)
            if first:
                acc[n] = value
            else:
                acc[n] += value

    def project_diag(i):
        forward[i].wait_recv()
        project(diag, i * size, size, False)

    def project_opp(i):
        project(opp, i * size, size, False)

    partner = peer(1)
    wanted = lax.shift_right_logical(prompt_ref[partner], 1)

    def pair(kind):
        return remote(
            stage.at[kind], landed.at[kind // 2, pl.ds((kind % 2) * part_len, part_len)],
            pair_send.at[kind], pair_recv.at[kind], (partner, tp),
        )

    def hand_over(kind):
        receive(kind, 3)
        stage[kind] = bufs[kind][wanted]
        pair(kind).start()

    lane = lax.broadcasted_iota(jnp.int32, (1, count), 1)
    token = lax.rem(lane, RMAX)
    owner_of = lax.div(lane, RMAX)
    group = count // RMAX
    shards = [shard_ref[seq * group + r] for r in range(group)]
    place = jnp.full((1, count), -1, jnp.int32)
    for r in range(group):
        rank = jnp.int32(0)
        for e in range(r):
            rank = rank + jnp.where(shards[e] == shards[r], 1, 0)
        slot = shards[r] * 2 + rank
        here = (owner_of == r) & (token < len_ref[seq * group + r])
        place = jnp.where(here, slot * RMAX + token, place)
    down = lax.broadcasted_iota(jnp.int32, (count, count), 0)
    deal = jnp.where(down == place, 1.0, 0.0).astype(bf16)
    valid[...] = jnp.broadcast_to(
        jnp.sum(deal.astype(f32), -1, keepdims=True), valid.shape
    )
    half = count // 2
    row = lax.broadcasted_iota(jnp.int32, (half, half), 0)
    col = lax.broadcasted_iota(jnp.int32, (half, half), 1)
    causal = (lax.div(row, RMAX) == lax.div(col, RMAX)) & (row >= col)

    for load in blocks[0]:
        load.wait()
    project(tp, 0, width, True)
    advance(1, (0, 1, 2, 3))
    relay(0)
    to_sib.wait_recv()
    for load in blocks[1]:
        load.wait()
    project(sib, 0, width, False)
    relay(1)
    advance(2, (0, 1))
    for i in (2, 3):
        for load in blocks[i]:
            load.wait()
    project_opp(0)
    project_diag(0)
    relay(2)
    project_opp(1)
    advance(2, (2, 3))
    project_diag(1)
    relay(3)
    project_opp(2)
    project_diag(2)
    hand_over(0)
    hand_over(1)
    project_opp(3)
    project_diag(3)
    relay(4)
    project_opp(4)
    hand_over(2)
    hand_over(3)
    project_diag(4)

    for table in tables:
        table.wait()
    cosine = cos_ref[...]
    sine = sin_ref[...]

    def turn(values):
        other = pltpu.roll(values, HD // 2, 1)
        shape = (count // RMAX, RMAX, HD)
        out = values.reshape(shape) * cosine[None] + other.reshape(shape) * sine[None]
        return out.reshape(count, HD).astype(bf16)

    for n in range(5):
        if n < 4:
            tile = jnp.concatenate([turn(acc[n, :, :HD]), turn(acc[n, :, HD:])], -1)
        else:
            tile = acc[n].astype(bf16)
        dealt[n] = jnp.dot(deal, tile, preferred_element_type=f32).astype(bf16)

    mine = prompt_ref[seq]
    here_too = lax.rem(mine, 2) == x
    scale = 1.0 / math.sqrt(HD)
    nt = (((1,), (1,)), ((), ()))

    def fetch(kind):
        pair(kind).wait_recv()
        part = slice((kind % 2) * part_len, (kind % 2 + 1) * part_len)
        landed[kind // 2, part] = jnp.where(
            here_too, bufs[kind][lax.shift_right_logical(mine, 1)], landed[kind // 2, part]
        )

    for kind in range(4):
        fetch(kind)

    def attend_rows(base):
        span_rows = pl.ds(base, half)
        mask = valid[span_rows, :1]
        for h in range(6):
            k = h // 3
            lanes = slice(k * HD, (k + 1) * HD)
            query = dealt[h // 2, span_rows, (h % 2) * HD:(h % 2 + 1) * HD]
            own_key = dealt[3, span_rows, lanes]
            own_value = dealt[4, span_rows, lanes]
            prior = lax.dot_general(query, landed[0, :, lanes], nt, preferred_element_type=f32)
            recent = lax.dot_general(query, own_key, nt, preferred_element_type=f32)
            prior = prior * scale
            recent = jnp.where(causal, recent * scale, -1e30)
            top = jnp.maximum(
                jnp.max(prior, -1, keepdims=True), jnp.max(recent, -1, keepdims=True)
            )
            prior, recent = jnp.exp(prior - top), jnp.exp(recent - top)
            total = jnp.sum(prior, -1, keepdims=True) + jnp.sum(recent, -1, keepdims=True)
            share = mask / total
            mixed = jnp.dot(
                (prior * share).astype(bf16), landed[1, :, lanes], preferred_element_type=f32
            ) + jnp.dot((recent * share).astype(bf16), own_value, preferred_element_type=f32)
            attn[span_rows, h * HD:(h + 1) * HD] = mixed.astype(bf16)

    def partial(owner, dst, base):
        span_rows = pl.ds(base, half)

        for n in range(width // 256):
            source = pl.ds(pl.multiple_of(owner * width + n * 256, 256), 256)
            dst[span_rows, n * 256:(n + 1) * 256] = jnp.dot(
                attn[span_rows], wo[:, source], preferred_element_type=f32
            ).astype(bf16)

    def swap(i, side):
        span_rows = pl.ds(bases[side], half)
        return remote(
            queue.at[i, span_rows], sibling.at[i, span_rows],
            sib_send.at[i, side], sib_recv.at[i, side], (seq, sib),
        )

    span = count // 8

    def chunk(m):
        return pl.ds(pl.multiple_of(peer(m) * span, span), span)

    def cross(m):
        return remote(
            ahead.at[chunk(m)], across.at[chunk(m)], cross_send.at[m], cross_recv.at[m], (seq, opp)
        )

    home = pl.ds(pl.multiple_of(seq * span, span), span)

    def deliver(m):
        return remote(
            done.at[chunk(m)], out_ref.at[home], out_send.at[m], out_recv.at[m], (peer(m), tp)
        )

    def accept(m):
        return remote(
            done.at[chunk(m)], out_ref.at[chunk(m)], out_send.at[m], out_recv.at[m], (peer(m), tp)
        )

    stay = pltpu.make_async_copy(done.at[home], out_ref.at[home], out_send.at[0])

    def pass_on(m):
        both = ahead[chunk(m)].astype(f32) + sibling[0, chunk(m)].astype(f32)
        ahead[chunk(m)] = both.astype(bf16)
        cross(m).start()

    def finish(m):
        cross(m).wait_recv()
        total = kept[chunk(m)].astype(f32) + sibling[1, chunk(m)].astype(f32)
        done[chunk(m)] = (total + across[chunk(m)].astype(f32)).astype(bf16)
        if m == 0:
            stay.start()
        else:
            deliver(m).start()

    bases = (
        pl.multiple_of((1 - z // 2) * half, half),
        pl.multiple_of((z // 2) * half, half),
    )
    wo_load.wait()
    attend_rows(bases[0])
    partial(diag, queue.at[0], bases[0])
    swap(0, 0).start()
    partial(opp, ahead, bases[0])
    partial(sib, queue.at[1], bases[0])
    swap(1, 0).start()
    swap(0, 0).wait_recv()
    for m in ORDER[:4]:
        pass_on(m)
    partial(tp, kept, bases[0])
    attend_rows(bases[1])
    swap(1, 0).wait_recv()
    finish(ORDER[0])
    partial(diag, queue.at[0], bases[1])
    swap(0, 1).start()
    partial(opp, ahead, bases[1])
    partial(sib, queue.at[1], bases[1])
    swap(1, 1).start()
    swap(0, 1).wait_recv()
    for m in ORDER[4:]:
        pass_on(m)
    finish(ORDER[1])
    partial(tp, kept, bases[1])
    finish(ORDER[2])
    finish(ORDER[3])
    swap(1, 1).wait_recv()
    for m in ORDER[4:]:
        finish(m)
    for m in ORDER[:-1]:
        accept(m).wait_recv()
    stay.wait()

    to_sib.wait_send()
    for i in range(PIECES):
        to_opp[i].wait_send()
        forward[i].wait_send()
    for kind in range(4):
        for step in range(3):
            for way in (0, 1):
                @pl.when(can_send(way, step))
                def _():
                    hop(kind, way, step).wait_send()
        pair(kind).wait_send()
    for i in (0, 1):
        for side in (0, 1):
            swap(i, side).wait_send()
    for m in range(8):
        cross(m).wait_send()
    for m in range(1, 8):
        deliver(m).wait_send()


def fused_device(resp_rows, resp_len, resp_shard, group_prompt, prompt_kv, w_query, w_keyval, w_out):
    group, tokens, width = resp_rows.shape
    count = group * tokens
    angles = np.arange(PL, PL + tokens, dtype=np.float32)[:, None] * (
        ROPE_BASE ** (-np.arange(0, HD, 2, dtype=np.float64) / HD)
    ).astype(np.float32)
    cosine = np.concatenate([np.cos(angles), np.cos(angles)], -1).astype(np.float32)
    sine = np.concatenate([-np.sin(angles), np.sin(angles)], -1).astype(np.float32)
    bf16 = jnp.bfloat16
    block = (count, width)
    smem = pl.BlockSpec(memory_space=pltpu.SMEM)
    hbm = pl.BlockSpec(memory_space=pl.ANY)
    dma = pltpu.SemaphoreType.DMA
    cache = (PL // 2, w_keyval.shape[2])
    out = pl.pallas_call(
        fused_kernel,
        out_shape=jax.ShapeDtypeStruct(block, bf16),
        in_specs=[smem] * 3 + [hbm] * 7,
        out_specs=hbm,
        scratch_shapes=[
            pltpu.VMEM(w_query.shape, bf16),
            pltpu.VMEM(w_keyval.shape, bf16),
            pltpu.VMEM(w_out.shape, bf16),
            pltpu.VMEM((4,) + block, bf16),
            pltpu.VMEM((5, count, 256), jnp.float32),
            pltpu.VMEM((tokens, HD), jnp.float32),
            pltpu.VMEM((tokens, HD), jnp.float32),
            pltpu.VMEM((4,) + cache, bf16),
            pltpu.VMEM((4,) + cache, bf16),
            pltpu.VMEM((4,) + cache, bf16),
            pltpu.VMEM((4,) + cache, bf16),
            pltpu.VMEM((4,) + cache, bf16),
            pltpu.VMEM((2, PL, w_keyval.shape[2]), bf16),
            pltpu.VMEM((5, count, 256), bf16),
            pltpu.VMEM((count, HD), jnp.float32),
            pltpu.VMEM((count, w_query.shape[1]), bf16),
            pltpu.VMEM((2,) + block, bf16),
            pltpu.VMEM((2,) + block, bf16),
            pltpu.VMEM(block, bf16),
            pltpu.VMEM(block, bf16),
            pltpu.VMEM(block, bf16),
            pltpu.VMEM(block, bf16),
            dma((16,)),
            dma((1 + 2 * PIECES,)),
            dma((1 + 2 * PIECES,)),
            dma((4, 2, 3)),
            dma((4, 4)),
            dma((4,)),
            dma((4,)),
            dma((2, 2)),
            dma((2, 2)),
            dma((8,)),
            dma((8,)),
            dma((8,)),
            dma((8,)),
        ],
        compiler_params=pltpu.CompilerParams(
            collective_id=0, has_side_effects=True, vmem_limit_bytes=56 * 1024 * 1024
        ),
        cost_estimate=pl.CostEstimate(
            flops=6 * 10**9, bytes_accessed=23 * 10**6, transcendentals=10**6
        ),
    )(
        resp_shard[:, 0], resp_len, group_prompt, jnp.asarray(cosine), jnp.asarray(sine),
        resp_rows.reshape(block), prompt_kv[:, 0], w_query, w_keyval, w_out,
    )
    return out.reshape(group, tokens, width)


def fits(mesh):
    return mesh.shape["seq"] == 8 and mesh.shape["tp"] == 4


def solution(mesh):
    return jax.shard_map(
        fused_device if fits(mesh) else per_device,
        mesh=mesh,
        in_specs=(
            P("seq", None, "tp"),
            P(),
            P(),
            P(),
            P(None, "seq", None, "tp"),
            P(None, "tp"),
            P(None, None, "tp"),
            P("tp", None),
        ),
        out_specs=P("seq", None, "tp"),
        check_vma=False,
    )
```

```python
import math

import jax
import jax.numpy as jnp
import numpy as np
from jax import lax
from jax.experimental import pallas as pl
from jax.experimental.pallas import tpu as pltpu
from jax.sharding import PartitionSpec as P

HD = 128
PL = 256
RMAX = 16


ROPE_BASE = 1000000.0


def rope_tables(count, width, offset):
    places = (offset + jnp.arange(count)).astype(jnp.float32)
    freqs = ROPE_BASE ** (-(jnp.arange(width // 2).astype(jnp.float32) * 2.0 / width))
    angles = places[:, None] * freqs[None, :]
    return (jnp.cos(angles), jnp.sin(angles))


def rotate(values, cosine, sine):
    half = values.shape[-1] // 2
    first = values[..., :half]
    second = values[..., half:]
    cosine = cosine[:, None, :]
    sine = sine[:, None, :]
    return jnp.concatenate([first * cosine - second * sine, second * cosine + first * sine], -1)


def attend(queries, own_keys, own_values, cached_keys, cached_values, lengths):
    scale = 1.0 / math.sqrt(queries.shape[-1])
    prior = (
        jnp.einsum("stkrh,pkh->krstp", queries, cached_keys, preferred_element_type=jnp.float32)
        * scale
    )
    recent = (
        jnp.einsum("stkrh,sukh->krstu", queries, own_keys, preferred_element_type=jnp.float32)
        * scale
    )
    places = jnp.arange(queries.shape[1])
    causal = places[:, None] >= places[None, :]
    recent = jnp.where(causal, recent, -1e30)
    top = jnp.maximum(jnp.max(prior, -1), jnp.max(recent, -1))
    prior_exp = jnp.exp(prior - top[..., None])
    recent_exp = jnp.exp(recent - top[..., None])
    total = jnp.sum(prior_exp, -1) + jnp.sum(recent_exp, -1)
    prior_w = (prior_exp / total[..., None]).astype(jnp.bfloat16)
    recent_w = (recent_exp / total[..., None]).astype(jnp.bfloat16)
    mixed = jnp.einsum(
        "krstp,pkh->stkrh", prior_w, cached_values, preferred_element_type=jnp.float32
    )
    mixed = mixed + jnp.einsum(
        "krstu,sukh->stkrh", recent_w, own_values, preferred_element_type=jnp.float32
    )
    valid = places[None, :] < lengths[:, None]
    mixed = jnp.where(valid[:, :, None, None, None], mixed, 0.0)
    return mixed.astype(jnp.bfloat16).reshape(queries.shape[0], queries.shape[1], -1)


def choose(match, capacity):
    group_size = match.shape[1]
    rank = jnp.cumsum(match.astype(jnp.int32), axis=1) - 1
    picked = match[:, None, :] & (rank[:, None, :] == jnp.arange(capacity)[None, :, None])
    chosen = jnp.sum(jnp.where(picked, jnp.arange(group_size)[None, None, :], 0), -1)
    filled = jnp.any(picked, -1)
    return (chosen.reshape(-1), filled.reshape(-1))


def outgoing(resp_len, resp_shard, group_size):
    learners = lax.axis_size("seq")
    group = lax.axis_index("seq")
    capacity = (group_size + learners - 1) // learners
    own = lax.dynamic_slice_in_dim(resp_shard[:, 0], group * group_size, group_size, 0)
    pick, filled = choose(own[None, :] == jnp.arange(learners)[:, None], capacity)
    lengths = jnp.where(filled, resp_len[group * group_size + pick], 0)
    return pick, lengths


def per_device(resp_rows, resp_len, resp_shard, group_prompt, prompt_kv, w_query, w_keyval, w_out):
    group = lax.axis_index("seq")
    pick, lengths = outgoing(resp_len, resp_shard, resp_rows.shape[0])
    caches = lax.all_gather(prompt_kv, "seq", axis=1, tiled=True)
    cache = lax.dynamic_index_in_dim(caches, group_prompt[group], 1, keepdims=False)
    features = lax.all_gather(jnp.take(resp_rows, pick, axis=0), "tp", axis=2, tiled=True)
    slots, token_count, width = features.shape
    flat = features.reshape(slots * token_count, width)
    kv_local = w_keyval.shape[2] // HD
    q_local = w_query.shape[1] // HD
    ratio = q_local // kv_local
    cosine, sine = rope_tables(token_count, HD, PL)
    queries = jnp.dot(flat, w_query, preferred_element_type=jnp.float32).reshape(
        slots, token_count, q_local, HD
    )
    queries = (
        rotate(queries, cosine, sine)
        .astype(jnp.bfloat16)
        .reshape(slots, token_count, kv_local, ratio, HD)
    )
    keys = jnp.dot(flat, w_keyval[0], preferred_element_type=jnp.float32)
    keys = rotate(keys.reshape(slots, token_count, kv_local, HD), cosine, sine)
    keys = keys.astype(jnp.bfloat16)
    values = jnp.dot(flat, w_keyval[1], preferred_element_type=jnp.float32).astype(jnp.bfloat16)
    values = values.reshape(slots, token_count, kv_local, HD)
    cached_keys = cache[0].reshape(-1, kv_local, HD)
    cached_values = cache[1].reshape(-1, kv_local, HD)
    attn = attend(queries, keys, values, cached_keys, cached_values, lengths)
    partial_value = jnp.dot(
        attn.reshape(-1, q_local * HD), w_out, preferred_element_type=jnp.float32
    ).astype(jnp.bfloat16)
    summed = lax.psum_scatter(
        partial_value.reshape(slots, token_count, -1), "tp", scatter_dimension=2, tiled=True
    )
    return lax.all_to_all(summed, "seq", split_axis=0, concat_axis=0, tiled=True)


MESH = pl.DeviceIdType.MESH
ORDER = (6, 7, 4, 5, 2, 3, 1, 0)
PIECES = 5


def fused_kernel(
    shard_ref, len_ref, prompt_ref, cos_hbm, sin_hbm, x_hbm, kv_hbm, wq_hbm, wkv_hbm, wo_hbm,
    out_ref,
    wq, wkv, wo, rows, acc, cos_ref, sin_ref, buf0, buf1, buf2, buf3, stage, landed, dealt, valid,
    attn, queue, sibling, ahead, kept, across, done,
    load_sem, gather_send, gather_recv, line_send, line_recv, pair_send, pair_recv,
    sib_send, sib_recv, cross_send, cross_recv, out_send, out_recv,
):
    seq = lax.axis_index("seq")
    tp = lax.axis_index("tp")
    z, x = seq // 2, seq % 2
    y, c = tp // 2, tp % 2
    sib = y * 2 + (1 - c)
    opp = (1 - y) * 2 + c
    diag = (1 - y) * 2 + (1 - c)
    count, width = x_hbm.shape
    f32, bf16 = jnp.float32, jnp.bfloat16
    bufs = (buf0, buf1, buf2, buf3)
    part_len = PL // 2

    def peer(m):
        zz = (z, z + 1 - 2 * (z % 2), z + 2 - 4 * (z // 2), 3 - z)[m // 2]
        return zz * 2 + (x, 1 - x)[m % 2]

    def local(src, dst, i):
        return pltpu.make_async_copy(src, dst, load_sem.at[i])

    x_load = local(x_hbm, rows.at[tp], 0)
    kv_loads = [
        local(kv_hbm.at[k // 2, pl.ds((k % 2) * part_len, part_len)], bufs[k].at[z], 1 + k)
        for k in range(4)
    ]
    tables = [local(cos_hbm, cos_ref, 5), local(sin_hbm, sin_ref, 6)]
    blocks = []
    for i, owner in enumerate((tp, sib, opp, diag)):
        part = pl.ds(pl.multiple_of(owner * width, width), width)
        blocks.append((
            local(wq_hbm.at[part], wq.at[part], 7 + 2 * i),
            local(wkv_hbm.at[:, part], wkv.at[:, part], 8 + 2 * i),
        ))
    wo_load = local(wo_hbm, wo, 15)
    for load in [x_load] + kv_loads + tables:
        load.start()
    def begin(i):
        for load in blocks[i]:
            load.start()

    def ready(i):
        for load in blocks[i]:
            load.wait()

    begin(0)

    barrier = pltpu.get_barrier_semaphore()
    for m in range(1, 8):
        pl.semaphore_signal(barrier, inc=1, device_id=(peer(m), tp), device_id_type=MESH)
    for other in (sib, opp):
        pl.semaphore_signal(barrier, inc=1, device_id=(seq, other), device_id_type=MESH)
    pl.semaphore_wait(barrier, 9)

    def remote(src, dst, send, recv, device):
        return pltpu.make_async_remote_copy(
            src_ref=src, dst_ref=dst, send_sem=send, recv_sem=recv,
            device_id=device, device_id_type=MESH,
        )

    size = width // PIECES
    to_sib = remote(rows.at[tp], rows.at[tp], gather_send.at[0], gather_recv.at[0], (seq, sib))
    to_opp, forward = [], []
    for i in range(PIECES):
        part = pl.ds(i * size, size)
        to_opp.append(
            remote(
                rows.at[tp, :, part], rows.at[tp, :, part],
                gather_send.at[1 + i], gather_recv.at[1 + i], (seq, opp),
            )
        )
        forward.append(
            remote(
                rows.at[opp, :, part], rows.at[opp, :, part],
                gather_send.at[1 + PIECES + i], gather_recv.at[1 + PIECES + i], (seq, sib),
            )
        )

    def hop(kind, way, step):
        block = z - step if way == 0 else z + step
        target = (z + 1 if way == 0 else z - 1) * 2 + x
        return remote(
            bufs[kind].at[block], bufs[kind].at[block],
            line_send.at[kind, way, step], line_recv.at[kind, block], (target, tp),
        )

    def can_send(way, step):
        return (z < 3) & (z >= step) if way == 0 else (z > 0) & (z + step <= 3)

    def has_source(way, step):
        return z >= step if way == 0 else z + step <= 3

    def launch(kind, step):
        for way in (0, 1):
            @pl.when(can_send(way, step))
            def _():
                hop(kind, way, step).start()

    def receive(kind, step):
        for way in (0, 1):
            @pl.when(has_source(way, step))
            def _():
                block = z - step if way == 0 else z + step
                remote(
                    bufs[kind].at[block], bufs[kind].at[block],
                    line_send.at[kind, way, 0], line_recv.at[kind, block], (seq, sib),
                ).wait_recv()

    x_load.wait()
    for copy in to_opp:
        copy.start()
    for kind in range(4):
        kv_loads[kind].wait()
        launch(kind, 0)
    to_sib.start()
    begin(1)

    def advance(step, kinds):
        for kind in kinds:
            receive(kind, step)
            launch(kind, step)

    def relay(i):
        to_opp[i].wait_recv()
        forward[i].start()

    def project(owner, start, depth, first):
        base = pl.multiple_of(owner * width + start, 256)
        source = rows[owner, :, start:start + depth]
        for n in range(5):
            if n < 3:
                weight = wq[pl.ds(base, depth), n * 256:(n + 1) * 256]
            else:
                weight = wkv[n - 3, pl.ds(base, depth), :]
            value = jnp.dot(source, weight, preferred_element_type=f32)
            if first:
                acc[n] = value
            else:
                acc[n] += value

    def project_diag(i):
        forward[i].wait_recv()
        project(diag, i * size, size, False)

    def project_opp(i):
        project(opp, i * size, size, False)

    partner = peer(1)
    wanted = lax.shift_right_logical(prompt_ref[partner], 1)

    def pair(kind):
        return remote(
            stage.at[kind], landed.at[kind // 2, pl.ds((kind % 2) * part_len, part_len)],
            pair_send.at[kind], pair_recv.at[kind], (partner, tp),
        )

    def hand_over(kind):
        receive(kind, 3)
        stage[kind] = bufs[kind][wanted]
        pair(kind).start()

    lane = lax.broadcasted_iota(jnp.int32, (1, count), 1)
    token = lax.rem(lane, RMAX)
    owner_of = lax.div(lane, RMAX)
    group = count // RMAX
    shards = [shard_ref[seq * group + r] for r in range(group)]
    place = jnp.full((1, count), -1, jnp.int32)
    for r in range(group):
        rank = jnp.int32(0)
        for e in range(r):
            rank = rank + jnp.where(shards[e] == shards[r], 1, 0)
        slot = shards[r] * 2 + rank
        here = (owner_of == r) & (token < len_ref[seq * group + r])
        place = jnp.where(here, slot * RMAX + token, place)
    down = lax.broadcasted_iota(jnp.int32, (count, count), 0)
    deal = jnp.where(down == place, 1.0, 0.0).astype(bf16)
    valid[...] = jnp.broadcast_to(
        jnp.sum(deal.astype(f32), -1, keepdims=True), valid.shape
    )
    half = count // 2
    row = lax.broadcasted_iota(jnp.int32, (half, half), 0)
    col = lax.broadcasted_iota(jnp.int32, (half, half), 1)
    causal = (lax.div(row, RMAX) == lax.div(col, RMAX)) & (row >= col)

    ready(0)
    begin(2)
    project(tp, 0, width, True)
    advance(1, (0, 1, 2, 3))
    relay(0)
    to_sib.wait_recv()
    ready(1)
    begin(3)
    project(sib, 0, width, False)
    relay(1)
    advance(2, (0, 1))
    ready(2)
    ready(3)
    wo_load.start()
    project_opp(0)
    project_diag(0)
    relay(2)
    project_opp(1)
    advance(2, (2, 3))
    project_diag(1)
    relay(3)
    project_opp(2)
    project_diag(2)
    hand_over(0)
    hand_over(1)
    project_opp(3)
    project_diag(3)
    relay(4)
    project_opp(4)
    hand_over(2)
    hand_over(3)
    project_diag(4)

    for table in tables:
        table.wait()
    cosine = cos_ref[...]
    sine = sin_ref[...]

    def turn(values):
        other = pltpu.roll(values, HD // 2, 1)
        shape = (count // RMAX, RMAX, HD)
        out = values.reshape(shape) * cosine[None] + other.reshape(shape) * sine[None]
        return out.reshape(count, HD).astype(bf16)

    for n in range(5):
        if n < 4:
            tile = jnp.concatenate([turn(acc[n, :, :HD]), turn(acc[n, :, HD:])], -1)
        else:
            tile = acc[n].astype(bf16)
        dealt[n] = jnp.dot(deal, tile, preferred_element_type=f32).astype(bf16)

    mine = prompt_ref[seq]
    here_too = lax.rem(mine, 2) == x
    scale = 1.0 / math.sqrt(HD)
    nt = (((1,), (1,)), ((), ()))

    def fetch(kind):
        pair(kind).wait_recv()
        part = slice((kind % 2) * part_len, (kind % 2 + 1) * part_len)
        landed[kind // 2, part] = jnp.where(
            here_too, bufs[kind][lax.shift_right_logical(mine, 1)], landed[kind // 2, part]
        )

    for kind in range(4):
        fetch(kind)

    def attend_rows(base):
        span_rows = pl.ds(base, half)
        mask = valid[span_rows, :1]
        for h in range(6):
            k = h // 3
            lanes = slice(k * HD, (k + 1) * HD)
            query = dealt[h // 2, span_rows, (h % 2) * HD:(h % 2 + 1) * HD]
            own_key = dealt[3, span_rows, lanes]
            own_value = dealt[4, span_rows, lanes]
            prior = lax.dot_general(query, landed[0, :, lanes], nt, preferred_element_type=f32)
            recent = lax.dot_general(query, own_key, nt, preferred_element_type=f32)
            prior = prior * scale
            recent = jnp.where(causal, recent * scale, -1e30)
            top = jnp.maximum(
                jnp.max(prior, -1, keepdims=True), jnp.max(recent, -1, keepdims=True)
            )
            prior, recent = jnp.exp(prior - top), jnp.exp(recent - top)
            total = jnp.sum(prior, -1, keepdims=True) + jnp.sum(recent, -1, keepdims=True)
            share = mask / total
            mixed = jnp.dot(
                (prior * share).astype(bf16), landed[1, :, lanes], preferred_element_type=f32
            ) + jnp.dot((recent * share).astype(bf16), own_value, preferred_element_type=f32)
            attn[span_rows, h * HD:(h + 1) * HD] = mixed.astype(bf16)

    def partial(owner, dst, base):
        span_rows = pl.ds(base, half)

        for n in range(width // 256):
            source = pl.ds(pl.multiple_of(owner * width + n * 256, 256), 256)
            dst[span_rows, n * 256:(n + 1) * 256] = jnp.dot(
                attn[span_rows], wo[:, source], preferred_element_type=f32
            ).astype(bf16)

    def swap(i, side):
        span_rows = pl.ds(bases[side], half)
        return remote(
            queue.at[i, span_rows], sibling.at[i, span_rows],
            sib_send.at[i, side], sib_recv.at[i, side], (seq, sib),
        )

    span = count // 8

    def chunk(m):
        return pl.ds(pl.multiple_of(peer(m) * span, span), span)

    def cross(m):
        return remote(
            ahead.at[chunk(m)], across.at[chunk(m)], cross_send.at[m], cross_recv.at[m], (seq, opp)
        )

    home = pl.ds(pl.multiple_of(seq * span, span), span)

    def deliver(m):
        return remote(
            done.at[chunk(m)], out_ref.at[home], out_send.at[m], out_recv.at[m], (peer(m), tp)
        )

    def accept(m):
        return remote(
            done.at[chunk(m)], out_ref.at[chunk(m)], out_send.at[m], out_recv.at[m], (peer(m), tp)
        )

    stay = pltpu.make_async_copy(done.at[home], out_ref.at[home], out_send.at[0])

    def pass_on(m):
        both = ahead[chunk(m)].astype(f32) + sibling[0, chunk(m)].astype(f32)
        ahead[chunk(m)] = both.astype(bf16)
        cross(m).start()

    def finish(m):
        cross(m).wait_recv()
        total = kept[chunk(m)].astype(f32) + sibling[1, chunk(m)].astype(f32)
        done[chunk(m)] = (total + across[chunk(m)].astype(f32)).astype(bf16)
        if m == 0:
            stay.start()
        else:
            deliver(m).start()

    bases = (
        pl.multiple_of((1 - z // 2) * half, half),
        pl.multiple_of((z // 2) * half, half),
    )
    wo_load.wait()
    attend_rows(bases[0])
    partial(diag, queue.at[0], bases[0])
    swap(0, 0).start()
    partial(opp, ahead, bases[0])
    partial(sib, queue.at[1], bases[0])
    swap(1, 0).start()
    swap(0, 0).wait_recv()
    for m in ORDER[:4]:
        pass_on(m)
    partial(tp, kept, bases[0])
    attend_rows(bases[1])
    swap(1, 0).wait_recv()
    finish(ORDER[0])
    partial(diag, queue.at[0], bases[1])
    swap(0, 1).start()
    partial(opp, ahead, bases[1])
    partial(sib, queue.at[1], bases[1])
    swap(1, 1).start()
    swap(0, 1).wait_recv()
    for m in ORDER[4:]:
        pass_on(m)
    finish(ORDER[1])
    partial(tp, kept, bases[1])
    finish(ORDER[2])
    finish(ORDER[3])
    swap(1, 1).wait_recv()
    for m in ORDER[4:]:
        finish(m)
    for m in ORDER[:-1]:
        accept(m).wait_recv()
    stay.wait()

    to_sib.wait_send()
    for i in range(PIECES):
        to_opp[i].wait_send()
        forward[i].wait_send()
    for kind in range(4):
        for step in range(3):
            for way in (0, 1):
                @pl.when(can_send(way, step))
                def _():
                    hop(kind, way, step).wait_send()
        pair(kind).wait_send()
    for i in (0, 1):
        for side in (0, 1):
            swap(i, side).wait_send()
    for m in range(8):
        cross(m).wait_send()
    for m in range(1, 8):
        deliver(m).wait_send()


def fused_device(resp_rows, resp_len, resp_shard, group_prompt, prompt_kv, w_query, w_keyval, w_out):
    group, tokens, width = resp_rows.shape
    count = group * tokens
    angles = np.arange(PL, PL + tokens, dtype=np.float32)[:, None] * (
        ROPE_BASE ** (-np.arange(0, HD, 2, dtype=np.float64) / HD)
    ).astype(np.float32)
    cosine = np.concatenate([np.cos(angles), np.cos(angles)], -1).astype(np.float32)
    sine = np.concatenate([-np.sin(angles), np.sin(angles)], -1).astype(np.float32)
    bf16 = jnp.bfloat16
    block = (count, width)
    smem = pl.BlockSpec(memory_space=pltpu.SMEM)
    hbm = pl.BlockSpec(memory_space=pl.ANY)
    dma = pltpu.SemaphoreType.DMA
    cache = (PL // 2, w_keyval.shape[2])
    out = pl.pallas_call(
        fused_kernel,
        out_shape=jax.ShapeDtypeStruct(block, bf16),
        in_specs=[smem] * 3 + [hbm] * 7,
        out_specs=hbm,
        scratch_shapes=[
            pltpu.VMEM(w_query.shape, bf16),
            pltpu.VMEM(w_keyval.shape, bf16),
            pltpu.VMEM(w_out.shape, bf16),
            pltpu.VMEM((4,) + block, bf16),
            pltpu.VMEM((5, count, 256), jnp.float32),
            pltpu.VMEM((tokens, HD), jnp.float32),
            pltpu.VMEM((tokens, HD), jnp.float32),
            pltpu.VMEM((4,) + cache, bf16),
            pltpu.VMEM((4,) + cache, bf16),
            pltpu.VMEM((4,) + cache, bf16),
            pltpu.VMEM((4,) + cache, bf16),
            pltpu.VMEM((4,) + cache, bf16),
            pltpu.VMEM((2, PL, w_keyval.shape[2]), bf16),
            pltpu.VMEM((5, count, 256), bf16),
            pltpu.VMEM((count, HD), jnp.float32),
            pltpu.VMEM((count, w_query.shape[1]), bf16),
            pltpu.VMEM((2,) + block, bf16),
            pltpu.VMEM((2,) + block, bf16),
            pltpu.VMEM(block, bf16),
            pltpu.VMEM(block, bf16),
            pltpu.VMEM(block, bf16),
            pltpu.VMEM(block, bf16),
            dma((16,)),
            dma((1 + 2 * PIECES,)),
            dma((1 + 2 * PIECES,)),
            dma((4, 2, 3)),
            dma((4, 4)),
            dma((4,)),
            dma((4,)),
            dma((2, 2)),
            dma((2, 2)),
            dma((8,)),
            dma((8,)),
            dma((8,)),
            dma((8,)),
        ],
        compiler_params=pltpu.CompilerParams(
            collective_id=0, has_side_effects=True, vmem_limit_bytes=56 * 1024 * 1024
        ),
        cost_estimate=pl.CostEstimate(
            flops=6 * 10**9, bytes_accessed=23 * 10**6, transcendentals=10**6
        ),
    )(
        resp_shard[:, 0], resp_len, group_prompt, jnp.asarray(cosine), jnp.asarray(sine),
        resp_rows.reshape(block), prompt_kv[:, 0], w_query, w_keyval, w_out,
    )
    return out.reshape(group, tokens, width)


def fits(mesh):
    return mesh.shape["seq"] == 8 and mesh.shape["tp"] == 4


def solution(mesh):
    return jax.shard_map(
        fused_device if fits(mesh) else per_device,
        mesh=mesh,
        in_specs=(
            P("seq", None, "tp"),
            P(),
            P(),
            P(),
            P(None, "seq", None, "tp"),
            P(None, "tp"),
            P(None, None, "tp"),
            P("tp", None),
        ),
        out_specs=P("seq", None, "tp"),
        check_vma=False,
    )
```

```python
import math

import jax
import jax.numpy as jnp
import numpy as np
from jax import lax
from jax.experimental import pallas as pl
from jax.experimental.pallas import tpu as pltpu
from jax.sharding import PartitionSpec as P

HD = 128
PL = 256
RMAX = 16


ROPE_BASE = 1000000.0


def rope_tables(count, width, offset):
    places = (offset + jnp.arange(count)).astype(jnp.float32)
    freqs = ROPE_BASE ** (-(jnp.arange(width // 2).astype(jnp.float32) * 2.0 / width))
    angles = places[:, None] * freqs[None, :]
    return (jnp.cos(angles), jnp.sin(angles))


def rotate(values, cosine, sine):
    half = values.shape[-1] // 2
    first = values[..., :half]
    second = values[..., half:]
    cosine = cosine[:, None, :]
    sine = sine[:, None, :]
    return jnp.concatenate([first * cosine - second * sine, second * cosine + first * sine], -1)


def attend(queries, own_keys, own_values, cached_keys, cached_values, lengths):
    scale = 1.0 / math.sqrt(queries.shape[-1])
    prior = (
        jnp.einsum("stkrh,pkh->krstp", queries, cached_keys, preferred_element_type=jnp.float32)
        * scale
    )
    recent = (
        jnp.einsum("stkrh,sukh->krstu", queries, own_keys, preferred_element_type=jnp.float32)
        * scale
    )
    places = jnp.arange(queries.shape[1])
    causal = places[:, None] >= places[None, :]
    recent = jnp.where(causal, recent, -1e30)
    top = jnp.maximum(jnp.max(prior, -1), jnp.max(recent, -1))
    prior_exp = jnp.exp(prior - top[..., None])
    recent_exp = jnp.exp(recent - top[..., None])
    total = jnp.sum(prior_exp, -1) + jnp.sum(recent_exp, -1)
    prior_w = (prior_exp / total[..., None]).astype(jnp.bfloat16)
    recent_w = (recent_exp / total[..., None]).astype(jnp.bfloat16)
    mixed = jnp.einsum(
        "krstp,pkh->stkrh", prior_w, cached_values, preferred_element_type=jnp.float32
    )
    mixed = mixed + jnp.einsum(
        "krstu,sukh->stkrh", recent_w, own_values, preferred_element_type=jnp.float32
    )
    valid = places[None, :] < lengths[:, None]
    mixed = jnp.where(valid[:, :, None, None, None], mixed, 0.0)
    return mixed.astype(jnp.bfloat16).reshape(queries.shape[0], queries.shape[1], -1)


def choose(match, capacity):
    group_size = match.shape[1]
    rank = jnp.cumsum(match.astype(jnp.int32), axis=1) - 1
    picked = match[:, None, :] & (rank[:, None, :] == jnp.arange(capacity)[None, :, None])
    chosen = jnp.sum(jnp.where(picked, jnp.arange(group_size)[None, None, :], 0), -1)
    filled = jnp.any(picked, -1)
    return (chosen.reshape(-1), filled.reshape(-1))


def outgoing(resp_len, resp_shard, group_size):
    learners = lax.axis_size("seq")
    group = lax.axis_index("seq")
    capacity = (group_size + learners - 1) // learners
    own = lax.dynamic_slice_in_dim(resp_shard[:, 0], group * group_size, group_size, 0)
    pick, filled = choose(own[None, :] == jnp.arange(learners)[:, None], capacity)
    lengths = jnp.where(filled, resp_len[group * group_size + pick], 0)
    return pick, lengths


def per_device(resp_rows, resp_len, resp_shard, group_prompt, prompt_kv, w_query, w_keyval, w_out):
    group = lax.axis_index("seq")
    pick, lengths = outgoing(resp_len, resp_shard, resp_rows.shape[0])
    caches = lax.all_gather(prompt_kv, "seq", axis=1, tiled=True)
    cache = lax.dynamic_index_in_dim(caches, group_prompt[group], 1, keepdims=False)
    features = lax.all_gather(jnp.take(resp_rows, pick, axis=0), "tp", axis=2, tiled=True)
    slots, token_count, width = features.shape
    flat = features.reshape(slots * token_count, width)
    kv_local = w_keyval.shape[2] // HD
    q_local = w_query.shape[1] // HD
    ratio = q_local // kv_local
    cosine, sine = rope_tables(token_count, HD, PL)
    queries = jnp.dot(flat, w_query, preferred_element_type=jnp.float32).reshape(
        slots, token_count, q_local, HD
    )
    queries = (
        rotate(queries, cosine, sine)
        .astype(jnp.bfloat16)
        .reshape(slots, token_count, kv_local, ratio, HD)
    )
    keys = jnp.dot(flat, w_keyval[0], preferred_element_type=jnp.float32)
    keys = rotate(keys.reshape(slots, token_count, kv_local, HD), cosine, sine)
    keys = keys.astype(jnp.bfloat16)
    values = jnp.dot(flat, w_keyval[1], preferred_element_type=jnp.float32).astype(jnp.bfloat16)
    values = values.reshape(slots, token_count, kv_local, HD)
    cached_keys = cache[0].reshape(-1, kv_local, HD)
    cached_values = cache[1].reshape(-1, kv_local, HD)
    attn = attend(queries, keys, values, cached_keys, cached_values, lengths)
    partial_value = jnp.dot(
        attn.reshape(-1, q_local * HD), w_out, preferred_element_type=jnp.float32
    ).astype(jnp.bfloat16)
    summed = lax.psum_scatter(
        partial_value.reshape(slots, token_count, -1), "tp", scatter_dimension=2, tiled=True
    )
    return lax.all_to_all(summed, "seq", split_axis=0, concat_axis=0, tiled=True)


MESH = pl.DeviceIdType.MESH
ORDER = (6, 7, 4, 5, 2, 3, 1, 0)
PIECES = 5


def fused_kernel(
    shard_ref, len_ref, prompt_ref, cos_hbm, sin_hbm, x_hbm, kv_hbm, wq_hbm, wkv_hbm, wo_hbm,
    out_ref,
    wq, wkv, wo, rows, acc, cos_ref, sin_ref, buf0, buf1, buf2, buf3, stage, landed, stacked, own, valid,
    attn, queue, sibling, ahead, kept, across, done,
    load_sem, gather_send, gather_recv, line_send, line_recv, pair_send, pair_recv,
    sib_send, sib_recv, cross_send, cross_recv, out_send, out_recv,
):
    seq = lax.axis_index("seq")
    tp = lax.axis_index("tp")
    z, x = seq // 2, seq % 2
    y, c = tp // 2, tp % 2
    sib = y * 2 + (1 - c)
    opp = (1 - y) * 2 + c
    diag = (1 - y) * 2 + (1 - c)
    count, width = x_hbm.shape
    f32, bf16 = jnp.float32, jnp.bfloat16
    bufs = (buf0, buf1, buf2, buf3)
    part_len = PL // 2

    def peer(m):
        zz = (z, z + 1 - 2 * (z % 2), z + 2 - 4 * (z // 2), 3 - z)[m // 2]
        return zz * 2 + (x, 1 - x)[m % 2]

    def local(src, dst, i):
        return pltpu.make_async_copy(src, dst, load_sem.at[i])

    x_load = local(x_hbm, rows.at[tp], 0)
    kv_loads = [
        local(kv_hbm.at[k // 2, pl.ds((k % 2) * part_len, part_len)], bufs[k].at[z], 1 + k)
        for k in range(4)
    ]
    tables = [local(cos_hbm, cos_ref, 5), local(sin_hbm, sin_ref, 6)]
    blocks = []
    for i, owner in enumerate((tp, sib, opp, diag)):
        part = pl.ds(pl.multiple_of(owner * width, width), width)
        blocks.append((
            local(wq_hbm.at[part], wq.at[part], 7 + 2 * i),
            local(wkv_hbm.at[:, part], wkv.at[:, part], 8 + 2 * i),
        ))
    wo_load = local(wo_hbm, wo, 15)
    for load in [x_load] + kv_loads + tables:
        load.start()
    for block in blocks:
        for load in block:
            load.start()
    wo_load.start()

    barrier = pltpu.get_barrier_semaphore()
    for m in range(1, 8):
        pl.semaphore_signal(barrier, inc=1, device_id=(peer(m), tp), device_id_type=MESH)
    for other in (sib, opp):
        pl.semaphore_signal(barrier, inc=1, device_id=(seq, other), device_id_type=MESH)
    pl.semaphore_wait(barrier, 9)

    def remote(src, dst, send, recv, device):
        return pltpu.make_async_remote_copy(
            src_ref=src, dst_ref=dst, send_sem=send, recv_sem=recv,
            device_id=device, device_id_type=MESH,
        )

    size = width // PIECES
    to_sib = remote(rows.at[tp], rows.at[tp], gather_send.at[0], gather_recv.at[0], (seq, sib))
    to_opp, forward = [], []
    for i in range(PIECES):
        part = pl.ds(i * size, size)
        to_opp.append(
            remote(
                rows.at[tp, :, part], rows.at[tp, :, part],
                gather_send.at[1 + i], gather_recv.at[1 + i], (seq, opp),
            )
        )
        forward.append(
            remote(
                rows.at[opp, :, part], rows.at[opp, :, part],
                gather_send.at[1 + PIECES + i], gather_recv.at[1 + PIECES + i], (seq, sib),
            )
        )

    def hop(kind, way, step):
        block = z - step if way == 0 else z + step
        target = (z + 1 if way == 0 else z - 1) * 2 + x
        return remote(
            bufs[kind].at[block], bufs[kind].at[block],
            line_send.at[kind, way, step], line_recv.at[kind, block], (target, tp),
        )

    def can_send(way, step):
        return (z < 3) & (z >= step) if way == 0 else (z > 0) & (z + step <= 3)

    def has_source(way, step):
        return z >= step if way == 0 else z + step <= 3

    def launch(kind, step):
        for way in (0, 1):
            @pl.when(can_send(way, step))
            def _():
                hop(kind, way, step).start()

    def receive(kind, step):
        for way in (0, 1):
            @pl.when(has_source(way, step))
            def _():
                block = z - step if way == 0 else z + step
                remote(
                    bufs[kind].at[block], bufs[kind].at[block],
                    line_send.at[kind, way, 0], line_recv.at[kind, block], (seq, sib),
                ).wait_recv()

    x_load.wait()
    for copy in to_opp:
        copy.start()
    for kind in (0, 1):
        kv_loads[kind].wait()
        launch(kind, 0)
    to_sib.start()

    def advance(step, kinds):
        for kind in kinds:
            receive(kind, step)
            launch(kind, step)

    def relay(i):
        to_opp[i].wait_recv()
        forward[i].start()

    def project(owner, start, depth, first):
        base = pl.multiple_of(owner * width + start, 256)
        source = rows[owner, :, start:start + depth]
        for n in range(5):
            if n < 3:
                weight = wq[pl.ds(base, depth), n * 256:(n + 1) * 256]
            else:
                weight = wkv[n - 3, pl.ds(base, depth), :]
            value = jnp.dot(source, weight, preferred_element_type=f32)
            if first:
                acc[n] = value
            else:
                acc[n] += value

    def project_diag(i):
        forward[i].wait_recv()
        project(diag, i * size, size, False)

    def project_opp(i):
        project(opp, i * size, size, False)

    partner = peer(1)
    wanted = lax.shift_right_logical(prompt_ref[partner], 1)

    def pair(kind):
        return remote(
            stage.at[kind], landed.at[kind // 2, pl.ds((kind % 2) * part_len, part_len)],
            pair_send.at[kind], pair_recv.at[kind], (partner, tp),
        )

    def hand_over(kind):
        receive(kind, 3)
        stage[kind] = bufs[kind][wanted]
        pair(kind).start()

    lane = lax.broadcasted_iota(jnp.int32, (1, count), 1)
    token = lax.rem(lane, RMAX)
    owner_of = lax.div(lane, RMAX)
    group = count // RMAX
    shards = [shard_ref[seq * group + r] for r in range(group)]
    place = jnp.full((1, count), -1, jnp.int32)
    for r in range(group):
        rank = jnp.int32(0)
        for e in range(r):
            rank = rank + jnp.where(shards[e] == shards[r], 1, 0)
        slot = shards[r] * 2 + rank
        here = (owner_of == r) & (token < len_ref[seq * group + r])
        place = jnp.where(here, slot * RMAX + token, place)
    down = lax.broadcasted_iota(jnp.int32, (count, count), 0)
    deal = jnp.where(down == place, 1.0, 0.0).astype(bf16)
    valid[...] = jnp.broadcast_to(
        jnp.sum(deal.astype(f32), -1, keepdims=True), valid.shape
    )
    half = count // 2
    row = lax.broadcasted_iota(jnp.int32, (half, half), 0)
    col = lax.broadcasted_iota(jnp.int32, (half, half), 1)
    causal = (lax.div(row, RMAX) == lax.div(col, RMAX)) & (row >= col)

    for load in blocks[0]:
        load.wait()
    project(tp, 0, width, True)
    advance(1, (0, 1))
    for kind in (2, 3):
        kv_loads[kind].wait()
        launch(kind, 0)
    relay(0)
    to_sib.wait_recv()
    for load in blocks[1]:
        load.wait()
    project(sib, 0, width, False)
    relay(1)
    advance(2, (0, 1))
    for i in (2, 3):
        for load in blocks[i]:
            load.wait()
    project_opp(0)
    advance(1, (2, 3))
    project_diag(0)
    relay(2)
    hand_over(0)
    hand_over(1)
    project_opp(1)
    project_diag(1)
    advance(2, (2, 3))
    relay(3)
    project_opp(2)
    project_diag(2)
    project_opp(3)
    project_diag(3)
    relay(4)
    project_opp(4)
    hand_over(2)
    hand_over(3)
    project_diag(4)

    for table in tables:
        table.wait()
    cosine = cos_ref[...]
    sine = sin_ref[...]

    def turn(values):
        other = pltpu.roll(values, HD // 2, 1)
        shape = (count // RMAX, RMAX, HD)
        out = values.reshape(shape) * cosine[None] + other.reshape(shape) * sine[None]
        return out.reshape(count, HD).astype(bf16)

    for n in range(5):
        if n < 4:
            tile = jnp.concatenate([turn(acc[n, :, :HD]), turn(acc[n, :, HD:])], -1)
        else:
            tile = acc[n].astype(bf16)
        tile = jnp.dot(deal, tile, preferred_element_type=f32).astype(bf16)
        for side in (0, 1):
            part = tile[side * half:(side + 1) * half]
            if n >= 3:
                own[n - 3, side] = part
                continue
            for j in (0, 1):
                head = 2 * n + j
                place_of = slice((head % 3) * half, (head % 3 + 1) * half)
                stacked[head // 3, side, place_of] = part[:, j * HD:(j + 1) * HD]

    mine = prompt_ref[seq]
    here_too = lax.rem(mine, 2) == x
    rate = math.log2(math.e) / math.sqrt(HD)
    nt = (((1,), (1,)), ((), ()))

    def fetch(kind):
        pair(kind).wait_recv()
        part = slice((kind % 2) * part_len, (kind % 2 + 1) * part_len)
        landed[kind // 2, part] = jnp.where(
            here_too, bufs[kind][lax.shift_right_logical(mine, 1)], landed[kind // 2, part]
        )

    def weigh(side, base, k):
        lanes = slice(k * HD, (k + 1) * HD)
        queries = stacked[k, side]
        prior_all = lax.dot_general(queries, landed[0, :, lanes], nt, preferred_element_type=f32)
        recent_all = lax.dot_general(queries, own[0, side, :, lanes], nt, preferred_element_type=f32)
        mask = valid[pl.ds(base, half), :1]
        priors, recents, shares = [], [], []
        for r in range(3):
            prior = prior_all[r * half:(r + 1) * half]
            recent = jnp.where(causal, recent_all[r * half:(r + 1) * half], -1e30)
            top = jnp.max(
                jnp.maximum(jnp.maximum(prior[:, :HD], prior[:, HD:]), recent), -1, keepdims=True
            )
            prior = jnp.exp2((prior - top) * rate)
            recent = jnp.exp2((recent - top) * rate)
            total = jnp.sum(prior[:, :HD] + prior[:, HD:] + recent, -1, keepdims=True)
            priors.append(prior.astype(bf16))
            recents.append(recent.astype(bf16))
            shares.append(mask / total)
        return jnp.concatenate(priors, 0), jnp.concatenate(recents, 0), shares

    def mix(side, base, k, weights):
        lanes = slice(k * HD, (k + 1) * HD)
        priors, recents, shares = weights
        mixed = jnp.dot(priors, landed[1, :, lanes], preferred_element_type=f32)
        mixed = mixed + jnp.dot(recents, own[1, side, :, lanes], preferred_element_type=f32)
        for r in range(3):
            head = 3 * k + r
            attn[pl.ds(base, half), head * HD:(head + 1) * HD] = (
                mixed[r * half:(r + 1) * half] * shares[r]
            ).astype(bf16)

    def partial(owner, dst, base):
        span_rows = pl.ds(base, half)

        for n in range(width // 256):
            source = pl.ds(pl.multiple_of(owner * width + n * 256, 256), 256)
            dst[span_rows, n * 256:(n + 1) * 256] = jnp.dot(
                attn[span_rows], wo[:, source], preferred_element_type=f32
            ).astype(bf16)

    def swap(i, side):
        span_rows = pl.ds(bases[side], half)
        return remote(
            queue.at[i, span_rows], sibling.at[i, span_rows],
            sib_send.at[i, side], sib_recv.at[i, side], (seq, sib),
        )

    span = count // 8

    def chunk(m):
        return pl.ds(pl.multiple_of(peer(m) * span, span), span)

    def cross(m):
        return remote(
            ahead.at[chunk(m)], across.at[chunk(m)], cross_send.at[m], cross_recv.at[m], (seq, opp)
        )

    home = pl.ds(pl.multiple_of(seq * span, span), span)

    def deliver(m):
        return remote(
            done.at[chunk(m)], out_ref.at[home], out_send.at[m], out_recv.at[m], (peer(m), tp)
        )

    def accept(m):
        return remote(
            done.at[chunk(m)], out_ref.at[chunk(m)], out_send.at[m], out_recv.at[m], (peer(m), tp)
        )

    stay = pltpu.make_async_copy(done.at[home], out_ref.at[home], out_send.at[0])

    def pass_on(m):
        both = ahead[chunk(m)].astype(f32) + sibling[0, chunk(m)].astype(f32)
        ahead[chunk(m)] = both.astype(bf16)
        cross(m).start()

    def finish(m):
        cross(m).wait_recv()
        total = kept[chunk(m)].astype(f32) + sibling[1, chunk(m)].astype(f32)
        done[chunk(m)] = (total + across[chunk(m)].astype(f32)).astype(bf16)
        if m == 0:
            stay.start()
        else:
            deliver(m).start()

    bases = (
        pl.multiple_of((1 - z // 2) * half, half),
        pl.multiple_of((z // 2) * half, half),
    )
    sides = (1 - z // 2, z // 2)
    fetch(0)
    fetch(1)
    first = weigh(sides[0], bases[0], 0)
    second = weigh(sides[0], bases[0], 1)
    fetch(2)
    fetch(3)
    mix(sides[0], bases[0], 0, first)
    mix(sides[0], bases[0], 1, second)
    wo_load.wait()
    partial(diag, queue.at[0], bases[0])
    swap(0, 0).start()
    partial(opp, ahead, bases[0])
    partial(sib, queue.at[1], bases[0])
    swap(1, 0).start()
    swap(0, 0).wait_recv()
    for m in ORDER[:4]:
        pass_on(m)
    partial(tp, kept, bases[0])
    mix(sides[1], bases[1], 0, weigh(sides[1], bases[1], 0))
    swap(1, 0).wait_recv()
    finish(ORDER[0])
    mix(sides[1], bases[1], 1, weigh(sides[1], bases[1], 1))
    finish(ORDER[1])
    partial(diag, queue.at[0], bases[1])
    swap(0, 1).start()
    partial(opp, ahead, bases[1])
    finish(ORDER[2])
    swap(0, 1).wait_recv()
    for m in ORDER[4:]:
        pass_on(m)
    finish(ORDER[3])
    partial(sib, queue.at[1], bases[1])
    swap(1, 1).start()
    partial(tp, kept, bases[1])
    swap(1, 1).wait_recv()
    for m in ORDER[4:]:
        finish(m)
    for m in ORDER[:-1]:
        accept(m).wait_recv()
    stay.wait()

    to_sib.wait_send()
    for i in range(PIECES):
        to_opp[i].wait_send()
        forward[i].wait_send()
    for kind in range(4):
        for step in range(3):
            for way in (0, 1):
                @pl.when(can_send(way, step))
                def _():
                    hop(kind, way, step).wait_send()
        pair(kind).wait_send()
    for i in (0, 1):
        for side in (0, 1):
            swap(i, side).wait_send()
    for m in range(8):
        cross(m).wait_send()
    for m in range(1, 8):
        deliver(m).wait_send()


def fused_device(resp_rows, resp_len, resp_shard, group_prompt, prompt_kv, w_query, w_keyval, w_out):
    group, tokens, width = resp_rows.shape
    count = group * tokens
    angles = np.arange(PL, PL + tokens, dtype=np.float32)[:, None] * (
        ROPE_BASE ** (-np.arange(0, HD, 2, dtype=np.float64) / HD)
    ).astype(np.float32)
    cosine = np.concatenate([np.cos(angles), np.cos(angles)], -1).astype(np.float32)
    sine = np.concatenate([-np.sin(angles), np.sin(angles)], -1).astype(np.float32)
    bf16 = jnp.bfloat16
    block = (count, width)
    smem = pl.BlockSpec(memory_space=pltpu.SMEM)
    hbm = pl.BlockSpec(memory_space=pl.ANY)
    dma = pltpu.SemaphoreType.DMA
    cache = (PL // 2, w_keyval.shape[2])
    out = pl.pallas_call(
        fused_kernel,
        out_shape=jax.ShapeDtypeStruct(block, bf16),
        in_specs=[smem] * 3 + [hbm] * 7,
        out_specs=hbm,
        scratch_shapes=[
            pltpu.VMEM(w_query.shape, bf16),
            pltpu.VMEM(w_keyval.shape, bf16),
            pltpu.VMEM(w_out.shape, bf16),
            pltpu.VMEM((4,) + block, bf16),
            pltpu.VMEM((5, count, 256), jnp.float32),
            pltpu.VMEM((tokens, HD), jnp.float32),
            pltpu.VMEM((tokens, HD), jnp.float32),
            pltpu.VMEM((4,) + cache, bf16),
            pltpu.VMEM((4,) + cache, bf16),
            pltpu.VMEM((4,) + cache, bf16),
            pltpu.VMEM((4,) + cache, bf16),
            pltpu.VMEM((4,) + cache, bf16),
            pltpu.VMEM((2, PL, w_keyval.shape[2]), bf16),
            pltpu.VMEM((2, 2, 3 * count // 2, HD), bf16),
            pltpu.VMEM((2, 2, count // 2, 256), bf16),
            pltpu.VMEM((count, HD), jnp.float32),
            pltpu.VMEM((count, w_query.shape[1]), bf16),
            pltpu.VMEM((2,) + block, bf16),
            pltpu.VMEM((2,) + block, bf16),
            pltpu.VMEM(block, bf16),
            pltpu.VMEM(block, bf16),
            pltpu.VMEM(block, bf16),
            pltpu.VMEM(block, bf16),
            dma((16,)),
            dma((1 + 2 * PIECES,)),
            dma((1 + 2 * PIECES,)),
            dma((4, 2, 3)),
            dma((4, 4)),
            dma((4,)),
            dma((4,)),
            dma((2, 2)),
            dma((2, 2)),
            dma((8,)),
            dma((8,)),
            dma((8,)),
            dma((8,)),
        ],
        compiler_params=pltpu.CompilerParams(
            collective_id=0, has_side_effects=True, vmem_limit_bytes=56 * 1024 * 1024
        ),
        cost_estimate=pl.CostEstimate(
            flops=6 * 10**9, bytes_accessed=23 * 10**6, transcendentals=10**6
        ),
    )(
        resp_shard[:, 0], resp_len, group_prompt, jnp.asarray(cosine), jnp.asarray(sine),
        resp_rows.reshape(block), prompt_kv[:, 0], w_query, w_keyval, w_out,
    )
    return out.reshape(group, tokens, width)


def fits(mesh):
    return mesh.shape["seq"] == 8 and mesh.shape["tp"] == 4


def solution(mesh):
    return jax.shard_map(
        fused_device if fits(mesh) else per_device,
        mesh=mesh,
        in_specs=(
            P("seq", None, "tp"),
            P(),
            P(),
            P(),
            P(None, "seq", None, "tp"),
            P(None, "tp"),
            P(None, None, "tp"),
            P("tp", None),
        ),
        out_specs=P("seq", None, "tp"),
        check_vma=False,
    )
```

```python
import math

import jax
import jax.numpy as jnp
import numpy as np
from jax import lax
from jax.experimental import pallas as pl
from jax.experimental.pallas import tpu as pltpu
from jax.sharding import PartitionSpec as P

HD = 128
PL = 256
RMAX = 16


ROPE_BASE = 1000000.0


def rope_tables(count, width, offset):
    places = (offset + jnp.arange(count)).astype(jnp.float32)
    freqs = ROPE_BASE ** (-(jnp.arange(width // 2).astype(jnp.float32) * 2.0 / width))
    angles = places[:, None] * freqs[None, :]
    return (jnp.cos(angles), jnp.sin(angles))


def rotate(values, cosine, sine):
    half = values.shape[-1] // 2
    first = values[..., :half]
    second = values[..., half:]
    cosine = cosine[:, None, :]
    sine = sine[:, None, :]
    return jnp.concatenate([first * cosine - second * sine, second * cosine + first * sine], -1)


def attend(queries, own_keys, own_values, cached_keys, cached_values, lengths):
    scale = 1.0 / math.sqrt(queries.shape[-1])
    prior = (
        jnp.einsum("stkrh,pkh->krstp", queries, cached_keys, preferred_element_type=jnp.float32)
        * scale
    )
    recent = (
        jnp.einsum("stkrh,sukh->krstu", queries, own_keys, preferred_element_type=jnp.float32)
        * scale
    )
    places = jnp.arange(queries.shape[1])
    causal = places[:, None] >= places[None, :]
    recent = jnp.where(causal, recent, -1e30)
    top = jnp.maximum(jnp.max(prior, -1), jnp.max(recent, -1))
    prior_exp = jnp.exp(prior - top[..., None])
    recent_exp = jnp.exp(recent - top[..., None])
    total = jnp.sum(prior_exp, -1) + jnp.sum(recent_exp, -1)
    prior_w = (prior_exp / total[..., None]).astype(jnp.bfloat16)
    recent_w = (recent_exp / total[..., None]).astype(jnp.bfloat16)
    mixed = jnp.einsum(
        "krstp,pkh->stkrh", prior_w, cached_values, preferred_element_type=jnp.float32
    )
    mixed = mixed + jnp.einsum(
        "krstu,sukh->stkrh", recent_w, own_values, preferred_element_type=jnp.float32
    )
    valid = places[None, :] < lengths[:, None]
    mixed = jnp.where(valid[:, :, None, None, None], mixed, 0.0)
    return mixed.astype(jnp.bfloat16).reshape(queries.shape[0], queries.shape[1], -1)


def choose(match, capacity):
    group_size = match.shape[1]
    rank = jnp.cumsum(match.astype(jnp.int32), axis=1) - 1
    picked = match[:, None, :] & (rank[:, None, :] == jnp.arange(capacity)[None, :, None])
    chosen = jnp.sum(jnp.where(picked, jnp.arange(group_size)[None, None, :], 0), -1)
    filled = jnp.any(picked, -1)
    return (chosen.reshape(-1), filled.reshape(-1))


def outgoing(resp_len, resp_shard, group_size):
    learners = lax.axis_size("seq")
    group = lax.axis_index("seq")
    capacity = (group_size + learners - 1) // learners
    own = lax.dynamic_slice_in_dim(resp_shard[:, 0], group * group_size, group_size, 0)
    pick, filled = choose(own[None, :] == jnp.arange(learners)[:, None], capacity)
    lengths = jnp.where(filled, resp_len[group * group_size + pick], 0)
    return pick, lengths


def per_device(resp_rows, resp_len, resp_shard, group_prompt, prompt_kv, w_query, w_keyval, w_out):
    group = lax.axis_index("seq")
    pick, lengths = outgoing(resp_len, resp_shard, resp_rows.shape[0])
    caches = lax.all_gather(prompt_kv, "seq", axis=1, tiled=True)
    cache = lax.dynamic_index_in_dim(caches, group_prompt[group], 1, keepdims=False)
    features = lax.all_gather(jnp.take(resp_rows, pick, axis=0), "tp", axis=2, tiled=True)
    slots, token_count, width = features.shape
    flat = features.reshape(slots * token_count, width)
    kv_local = w_keyval.shape[2] // HD
    q_local = w_query.shape[1] // HD
    ratio = q_local // kv_local
    cosine, sine = rope_tables(token_count, HD, PL)
    queries = jnp.dot(flat, w_query, preferred_element_type=jnp.float32).reshape(
        slots, token_count, q_local, HD
    )
    queries = (
        rotate(queries, cosine, sine)
        .astype(jnp.bfloat16)
        .reshape(slots, token_count, kv_local, ratio, HD)
    )
    keys = jnp.dot(flat, w_keyval[0], preferred_element_type=jnp.float32)
    keys = rotate(keys.reshape(slots, token_count, kv_local, HD), cosine, sine)
    keys = keys.astype(jnp.bfloat16)
    values = jnp.dot(flat, w_keyval[1], preferred_element_type=jnp.float32).astype(jnp.bfloat16)
    values = values.reshape(slots, token_count, kv_local, HD)
    cached_keys = cache[0].reshape(-1, kv_local, HD)
    cached_values = cache[1].reshape(-1, kv_local, HD)
    attn = attend(queries, keys, values, cached_keys, cached_values, lengths)
    partial_value = jnp.dot(
        attn.reshape(-1, q_local * HD), w_out, preferred_element_type=jnp.float32
    ).astype(jnp.bfloat16)
    summed = lax.psum_scatter(
        partial_value.reshape(slots, token_count, -1), "tp", scatter_dimension=2, tiled=True
    )
    return lax.all_to_all(summed, "seq", split_axis=0, concat_axis=0, tiled=True)


MESH = pl.DeviceIdType.MESH
ORDER = (6, 7, 4, 5, 2, 3, 1, 0)
PIECES = 5


def fused_kernel(
    shard_ref, len_ref, prompt_ref, cos_hbm, sin_hbm, x_hbm, kv_hbm, wq_hbm, wkv_hbm, wo_hbm,
    out_ref,
    wq, wkv, wo, rows, acc, cos_ref, sin_ref, buf0, buf1, buf2, buf3, stage, landed, stacked, own, valid,
    attn, queue, sibling, ahead, kept, across, done,
    load_sem, gather_send, gather_recv, line_send, line_recv, pair_send, pair_recv,
    sib_send, sib_recv, cross_send, cross_recv, out_send, out_recv,
):
    seq = lax.axis_index("seq")
    tp = lax.axis_index("tp")
    z, x = seq // 2, seq % 2
    y, c = tp // 2, tp % 2
    sib = y * 2 + (1 - c)
    opp = (1 - y) * 2 + c
    diag = (1 - y) * 2 + (1 - c)
    count, width = x_hbm.shape
    f32, bf16 = jnp.float32, jnp.bfloat16
    bufs = (buf0, buf1, buf2, buf3)
    part_len = PL // 2

    def peer(m):
        zz = (z, z + 1 - 2 * (z % 2), z + 2 - 4 * (z // 2), 3 - z)[m // 2]
        return zz * 2 + (x, 1 - x)[m % 2]

    def local(src, dst, i):
        return pltpu.make_async_copy(src, dst, load_sem.at[i])

    x_load = local(x_hbm, rows.at[tp], 0)
    kv_loads = [
        local(kv_hbm.at[k // 2, pl.ds((k % 2) * part_len, part_len)], bufs[k].at[z], 1 + k)
        for k in range(4)
    ]
    tables = [local(cos_hbm, cos_ref, 5), local(sin_hbm, sin_ref, 6)]
    blocks = []
    for i, owner in enumerate((tp, sib, opp, diag)):
        part = pl.ds(pl.multiple_of(owner * width, width), width)
        blocks.append((
            local(wq_hbm.at[part], wq.at[part], 7 + 2 * i),
            local(wkv_hbm.at[:, part], wkv.at[:, part], 8 + 2 * i),
        ))
    wo_load = local(wo_hbm, wo, 15)
    for load in [x_load] + kv_loads + tables:
        load.start()
    for block in blocks:
        for load in block:
            load.start()
    wo_load.start()

    barrier = pltpu.get_barrier_semaphore()
    for m in range(1, 8):
        pl.semaphore_signal(barrier, inc=1, device_id=(peer(m), tp), device_id_type=MESH)
    for other in (sib, opp):
        pl.semaphore_signal(barrier, inc=1, device_id=(seq, other), device_id_type=MESH)
    pl.semaphore_wait(barrier, 9)

    def remote(src, dst, send, recv, device):
        return pltpu.make_async_remote_copy(
            src_ref=src, dst_ref=dst, send_sem=send, recv_sem=recv,
            device_id=device, device_id_type=MESH,
        )

    size = width // PIECES
    to_sib = remote(rows.at[tp], rows.at[tp], gather_send.at[0], gather_recv.at[0], (seq, sib))
    to_opp, forward = [], []
    for i in range(PIECES):
        part = pl.ds(i * size, size)
        to_opp.append(
            remote(
                rows.at[tp, :, part], rows.at[tp, :, part],
                gather_send.at[1 + i], gather_recv.at[1 + i], (seq, opp),
            )
        )
        forward.append(
            remote(
                rows.at[opp, :, part], rows.at[opp, :, part],
                gather_send.at[1 + PIECES + i], gather_recv.at[1 + PIECES + i], (seq, sib),
            )
        )

    def hop(kind, way, step):
        block = z - step if way == 0 else z + step
        target = (z + 1 if way == 0 else z - 1) * 2 + x
        return remote(
            bufs[kind].at[block], bufs[kind].at[block],
            line_send.at[kind, way, step], line_recv.at[kind, block], (target, tp),
        )

    def can_send(way, step):
        return (z < 3) & (z >= step) if way == 0 else (z > 0) & (z + step <= 3)

    def has_source(way, step):
        return z >= step if way == 0 else z + step <= 3

    def launch(kind, step):
        for way in (0, 1):
            @pl.when(can_send(way, step))
            def _():
                hop(kind, way, step).start()

    def receive(kind, step):
        for way in (0, 1):
            @pl.when(has_source(way, step))
            def _():
                block = z - step if way == 0 else z + step
                remote(
                    bufs[kind].at[block], bufs[kind].at[block],
                    line_send.at[kind, way, 0], line_recv.at[kind, block], (seq, sib),
                ).wait_recv()

    x_load.wait()
    for copy in to_opp:
        copy.start()
    for kind in (0, 1):
        kv_loads[kind].wait()
        launch(kind, 0)
    to_sib.start()

    def advance(step, kinds):
        for kind in kinds:
            receive(kind, step)
            launch(kind, step)

    def relay(i):
        to_opp[i].wait_recv()
        forward[i].start()

    def project(owner, start, depth, first):
        base = pl.multiple_of(owner * width + start, 256)
        source = rows[owner, :, start:start + depth]
        for n in range(5):
            if n < 3:
                weight = wq[pl.ds(base, depth), n * 256:(n + 1) * 256]
            else:
                weight = wkv[n - 3, pl.ds(base, depth), :]
            value = jnp.dot(source, weight, preferred_element_type=f32)
            if first:
                acc[n] = value
            else:
                acc[n] += value

    def project_diag(i):
        forward[i].wait_recv()
        project(diag, i * size, size, False)

    def project_opp(i):
        project(opp, i * size, size, False)

    partner = peer(1)
    wanted = lax.shift_right_logical(prompt_ref[partner], 1)

    def pair(kind):
        return remote(
            stage.at[kind], landed.at[kind // 2, pl.ds((kind % 2) * part_len, part_len)],
            pair_send.at[kind], pair_recv.at[kind], (partner, tp),
        )

    def hand_over(kind):
        receive(kind, 3)
        stage[kind] = bufs[kind][wanted]
        pair(kind).start()

    lane = lax.broadcasted_iota(jnp.int32, (1, count), 1)
    token = lax.rem(lane, RMAX)
    owner_of = lax.div(lane, RMAX)
    group = count // RMAX
    shards = [shard_ref[seq * group + r] for r in range(group)]
    place = jnp.full((1, count), -1, jnp.int32)
    for r in range(group):
        rank = jnp.int32(0)
        for e in range(r):
            rank = rank + jnp.where(shards[e] == shards[r], 1, 0)
        slot = shards[r] * 2 + rank
        here = (owner_of == r) & (token < len_ref[seq * group + r])
        place = jnp.where(here, slot * RMAX + token, place)
    down = lax.broadcasted_iota(jnp.int32, (count, count), 0)
    deal = jnp.where(down == place, 1.0, 0.0).astype(bf16)
    valid[...] = jnp.broadcast_to(
        jnp.sum(deal.astype(f32), -1, keepdims=True), valid.shape
    )
    half = count // 2
    row = lax.broadcasted_iota(jnp.int32, (half, half), 0)
    col = lax.broadcasted_iota(jnp.int32, (half, half), 1)
    causal = (lax.div(row, RMAX) == lax.div(col, RMAX)) & (row >= col)

    for load in blocks[0]:
        load.wait()
    project(tp, 0, width, True)
    advance(1, (0, 1))
    for kind in (2, 3):
        kv_loads[kind].wait()
        launch(kind, 0)
    relay(0)
    to_sib.wait_recv()
    for load in blocks[1]:
        load.wait()
    project(sib, 0, width, False)
    relay(1)
    advance(2, (0, 1))
    for i in (2, 3):
        for load in blocks[i]:
            load.wait()
    project_opp(0)
    advance(1, (2, 3))
    project_diag(0)
    relay(2)
    hand_over(0)
    hand_over(1)
    project_opp(1)
    project_diag(1)
    advance(2, (2, 3))
    relay(3)
    project_opp(2)
    project_diag(2)
    project_opp(3)
    project_diag(3)
    relay(4)
    project_opp(4)
    hand_over(2)
    hand_over(3)
    project_diag(4)

    for table in tables:
        table.wait()
    cosine = cos_ref[...]
    sine = sin_ref[...]

    def turn(values):
        other = pltpu.roll(values, HD // 2, 1)
        shape = (count // RMAX, RMAX, HD)
        out = values.reshape(shape) * cosine[None] + other.reshape(shape) * sine[None]
        return out.reshape(count, HD).astype(bf16)

    for n in range(5):
        if n < 4:
            tile = jnp.concatenate([turn(acc[n, :, :HD]), turn(acc[n, :, HD:])], -1)
        else:
            tile = acc[n].astype(bf16)
        tile = jnp.dot(deal, tile, preferred_element_type=f32).astype(bf16)
        for side in (0, 1):
            part = tile[side * half:(side + 1) * half]
            if n >= 3:
                own[n - 3, side] = part
                continue
            for j in (0, 1):
                head = 2 * n + j
                place_of = slice((head % 3) * half, (head % 3 + 1) * half)
                stacked[head // 3, side, place_of] = part[:, j * HD:(j + 1) * HD]

    mine = prompt_ref[seq]
    here_too = lax.rem(mine, 2) == x
    rate = math.log2(math.e) / math.sqrt(HD)
    nt = (((1,), (1,)), ((), ()))

    def fetch(kind):
        pair(kind).wait_recv()
        part = slice((kind % 2) * part_len, (kind % 2 + 1) * part_len)
        landed[kind // 2, part] = jnp.where(
            here_too, bufs[kind][lax.shift_right_logical(mine, 1)], landed[kind // 2, part]
        )

    def weigh(side, base, k):
        lanes = slice(k * HD, (k + 1) * HD)
        queries = stacked[k, side]
        prior_all = lax.dot_general(queries, landed[0, :, lanes], nt, preferred_element_type=f32)
        recent_all = lax.dot_general(queries, own[0, side, :, lanes], nt, preferred_element_type=f32)
        mask = valid[pl.ds(base, half), :1]
        priors, recents, shares = [], [], []
        for r in range(3):
            prior = prior_all[r * half:(r + 1) * half]
            recent = jnp.where(causal, recent_all[r * half:(r + 1) * half], -1e30)
            top = jnp.max(
                jnp.maximum(jnp.maximum(prior[:, :HD], prior[:, HD:]), recent), -1, keepdims=True
            )
            prior = jnp.exp2((prior - top) * rate)
            recent = jnp.exp2((recent - top) * rate)
            total = jnp.sum(prior[:, :HD] + prior[:, HD:] + recent, -1, keepdims=True)
            priors.append(prior.astype(bf16))
            recents.append(recent.astype(bf16))
            shares.append(mask / total)
        return jnp.concatenate(priors, 0), jnp.concatenate(recents, 0), shares

    def mix(side, base, k, weights):
        lanes = slice(k * HD, (k + 1) * HD)
        priors, recents, shares = weights
        mixed = jnp.dot(priors, landed[1, :, lanes], preferred_element_type=f32)
        mixed = mixed + jnp.dot(recents, own[1, side, :, lanes], preferred_element_type=f32)
        for r in range(3):
            head = 3 * k + r
            attn[pl.ds(base, half), head * HD:(head + 1) * HD] = (
                mixed[r * half:(r + 1) * half] * shares[r]
            ).astype(bf16)

    def partial(owner, dst, base):
        span_rows = pl.ds(base, half)

        for n in range(width // 256):
            source = pl.ds(pl.multiple_of(owner * width + n * 256, 256), 256)
            dst[span_rows, n * 256:(n + 1) * 256] = jnp.dot(
                attn[span_rows], wo[:, source], preferred_element_type=f32
            ).astype(bf16)

    def swap(i, side):
        span_rows = pl.ds(bases[side], half)
        return remote(
            queue.at[i, span_rows], sibling.at[i, span_rows],
            sib_send.at[i, side], sib_recv.at[i, side], (seq, sib),
        )

    span = count // 8

    def chunk(m):
        return pl.ds(pl.multiple_of(peer(m) * span, span), span)

    def cross(m):
        return remote(
            ahead.at[chunk(m)], across.at[chunk(m)], cross_send.at[m], cross_recv.at[m], (seq, opp)
        )

    home = pl.ds(pl.multiple_of(seq * span, span), span)

    def deliver(m):
        return remote(
            done.at[chunk(m)], out_ref.at[home], out_send.at[m], out_recv.at[m], (peer(m), tp)
        )

    def accept(m):
        return remote(
            done.at[chunk(m)], out_ref.at[chunk(m)], out_send.at[m], out_recv.at[m], (peer(m), tp)
        )

    stay = pltpu.make_async_copy(done.at[home], out_ref.at[home], out_send.at[0])

    def pass_on(m):
        both = ahead[chunk(m)].astype(f32) + sibling[0, chunk(m)].astype(f32)
        ahead[chunk(m)] = both.astype(bf16)
        cross(m).start()

    def finish(m):
        cross(m).wait_recv()
        total = kept[chunk(m)].astype(f32) + sibling[1, chunk(m)].astype(f32)
        done[chunk(m)] = (total + across[chunk(m)].astype(f32)).astype(bf16)
        if m == 0:
            stay.start()
        else:
            deliver(m).start()

    bases = (
        pl.multiple_of((1 - z // 2) * half, half),
        pl.multiple_of((z // 2) * half, half),
    )
    sides = (1 - z // 2, z // 2)
    fetch(0)
    fetch(1)
    first = weigh(sides[0], bases[0], 0)
    second = weigh(sides[0], bases[0], 1)
    fetch(2)
    fetch(3)
    mix(sides[0], bases[0], 0, first)
    mix(sides[0], bases[0], 1, second)
    wo_load.wait()
    partial(diag, queue.at[0], bases[0])
    swap(0, 0).start()
    partial(opp, ahead, bases[0])
    partial(sib, queue.at[1], bases[0])
    swap(1, 0).start()
    swap(0, 0).wait_recv()
    for m in ORDER[:4]:
        pass_on(m)
    partial(tp, kept, bases[0])
    swap(1, 0).wait_recv()
    finish(ORDER[0])
    mix(sides[1], bases[1], 0, weigh(sides[1], bases[1], 0))
    finish(ORDER[1])
    mix(sides[1], bases[1], 1, weigh(sides[1], bases[1], 1))
    finish(ORDER[2])
    partial(diag, queue.at[0], bases[1])
    swap(0, 1).start()
    finish(ORDER[3])
    partial(opp, ahead, bases[1])
    swap(0, 1).wait_recv()
    for m in ORDER[4:]:
        pass_on(m)
    partial(sib, queue.at[1], bases[1])
    swap(1, 1).start()
    partial(tp, kept, bases[1])
    swap(1, 1).wait_recv()
    for m in ORDER[4:]:
        finish(m)
    for m in ORDER[:-1]:
        accept(m).wait_recv()
    stay.wait()

    to_sib.wait_send()
    for i in range(PIECES):
        to_opp[i].wait_send()
        forward[i].wait_send()
    for kind in range(4):
        for step in range(3):
            for way in (0, 1):
                @pl.when(can_send(way, step))
                def _():
                    hop(kind, way, step).wait_send()
        pair(kind).wait_send()
    for i in (0, 1):
        for side in (0, 1):
            swap(i, side).wait_send()
    for m in range(8):
        cross(m).wait_send()
    for m in range(1, 8):
        deliver(m).wait_send()


def fused_device(resp_rows, resp_len, resp_shard, group_prompt, prompt_kv, w_query, w_keyval, w_out):
    group, tokens, width = resp_rows.shape
    count = group * tokens
    angles = np.arange(PL, PL + tokens, dtype=np.float32)[:, None] * (
        ROPE_BASE ** (-np.arange(0, HD, 2, dtype=np.float64) / HD)
    ).astype(np.float32)
    cosine = np.concatenate([np.cos(angles), np.cos(angles)], -1).astype(np.float32)
    sine = np.concatenate([-np.sin(angles), np.sin(angles)], -1).astype(np.float32)
    bf16 = jnp.bfloat16
    block = (count, width)
    smem = pl.BlockSpec(memory_space=pltpu.SMEM)
    hbm = pl.BlockSpec(memory_space=pl.ANY)
    dma = pltpu.SemaphoreType.DMA
    cache = (PL // 2, w_keyval.shape[2])
    out = pl.pallas_call(
        fused_kernel,
        out_shape=jax.ShapeDtypeStruct(block, bf16),
        in_specs=[smem] * 3 + [hbm] * 7,
        out_specs=hbm,
        scratch_shapes=[
            pltpu.VMEM(w_query.shape, bf16),
            pltpu.VMEM(w_keyval.shape, bf16),
            pltpu.VMEM(w_out.shape, bf16),
            pltpu.VMEM((4,) + block, bf16),
            pltpu.VMEM((5, count, 256), jnp.float32),
            pltpu.VMEM((tokens, HD), jnp.float32),
            pltpu.VMEM((tokens, HD), jnp.float32),
            pltpu.VMEM((4,) + cache, bf16),
            pltpu.VMEM((4,) + cache, bf16),
            pltpu.VMEM((4,) + cache, bf16),
            pltpu.VMEM((4,) + cache, bf16),
            pltpu.VMEM((4,) + cache, bf16),
            pltpu.VMEM((2, PL, w_keyval.shape[2]), bf16),
            pltpu.VMEM((2, 2, 3 * count // 2, HD), bf16),
            pltpu.VMEM((2, 2, count // 2, 256), bf16),
            pltpu.VMEM((count, HD), jnp.float32),
            pltpu.VMEM((count, w_query.shape[1]), bf16),
            pltpu.VMEM((2,) + block, bf16),
            pltpu.VMEM((2,) + block, bf16),
            pltpu.VMEM(block, bf16),
            pltpu.VMEM(block, bf16),
            pltpu.VMEM(block, bf16),
            pltpu.VMEM(block, bf16),
            dma((16,)),
            dma((1 + 2 * PIECES,)),
            dma((1 + 2 * PIECES,)),
            dma((4, 2, 3)),
            dma((4, 4)),
            dma((4,)),
            dma((4,)),
            dma((2, 2)),
            dma((2, 2)),
            dma((8,)),
            dma((8,)),
            dma((8,)),
            dma((8,)),
        ],
        compiler_params=pltpu.CompilerParams(
            collective_id=0, has_side_effects=True, vmem_limit_bytes=56 * 1024 * 1024
        ),
        cost_estimate=pl.CostEstimate(
            flops=6 * 10**9, bytes_accessed=23 * 10**6, transcendentals=10**6
        ),
    )(
        resp_shard[:, 0], resp_len, group_prompt, jnp.asarray(cosine), jnp.asarray(sine),
        resp_rows.reshape(block), prompt_kv[:, 0], w_query, w_keyval, w_out,
    )
    return out.reshape(group, tokens, width)


def fits(mesh):
    return mesh.shape["seq"] == 8 and mesh.shape["tp"] == 4


def solution(mesh):
    return jax.shard_map(
        fused_device if fits(mesh) else per_device,
        mesh=mesh,
        in_specs=(
            P("seq", None, "tp"),
            P(),
            P(),
            P(),
            P(None, "seq", None, "tp"),
            P(None, "tp"),
            P(None, None, "tp"),
            P("tp", None),
        ),
        out_specs=P("seq", None, "tp"),
        check_vma=False,
    )
```
